512 devices in a mesh: dp: 4 (over x), ctx: 4 (over y_lo), vocab: 32 (over y_hi, z, core).
Axes of the slice: x: 4, y: 8 (y_hi: 2, y_lo: 4; y = y_hi * 4 + y_lo), z: 8, core: 2. Of those that a mesh axis runs over, the one named last changes fastest.
Arguments:
- hidden: bfloat16 [4, 256, 2048], P('dp', 'ctx'), may hold values from -32 to 32
- head_weight: bfloat16 [114688, 2048], P(('ctx', 'vocab')), may hold values from -12 to 12
- labels: int32 [4, 256], P('dp'), may hold values from 0 to 114687
- loss_mask: int32 [4, 256], P('dp'), may hold values from 0 to 1
- seq_ids: int32 [4, 256], P('dp'), may hold values from 0 to 7, as said below
- old_logp: float32 [4, 256], P('dp'), may hold values from -20 to 0
- ref_logp: float32 [4, 256], P('dp'), may hold values from -20 to -13.5
- advantages: float32 [4, 8], P('dp'), may hold values from -4 to 4
Outputs:
- hidden_grad: bfloat16 [4, 256, 2048], P('dp', 'ctx', 'vocab')
- head_grad: bfloat16 [114688, 2048], P(('ctx', 'vocab'), 'dp')
The draws below stay inside these ranges and needn't reach their ends.
Inputs may be any that keep to these rules, and one draw needn't show every extreme that they name: seq_ids never fall along a window, and every sequence number from 0 to 7 occurs in each window.
All inputs are finite; a program needn't handle non-finite values.
Results may differ from the reference program's by a relative error of at most 0.035.
Values may be sent and summed in bfloat16 or wider, within the bound.
A program may use at most 64 MiB of HBM per device.

```python
import math
import jax
import jax.numpy as jnp
from jax import lax

D = 2048
SEQS = 8
GROUPS = 4
WINDOW = 256
VOCAB = 114688


def shift_dir(key):
    folded = jax.random.fold_in(key, 902)
    return jax.random.truncated_normal(folded, -3.0, 3.0, (D,), jnp.float32) / math.sqrt(D)


def drawn_spots():
    total_rows = GROUPS * WINDOW
    stride = total_rows // 12
    spots = jnp.array([i * stride for i in range(12)], jnp.int32)
    targets = jnp.array([i % 4 * (VOCAB // 4) for i in range(12)], jnp.int32)
    return (spots, targets)


def draw_head_weight(key, part):
    lifted = shift_dir(key)
    key = jax.random.fold_in(key, 11)
    positions = jnp.arange(VOCAB, dtype=jnp.float32) / VOCAB
    base = jax.random.truncated_normal(key, -5.0, 5.0, (VOCAB, D), jnp.float32)
    scales = 3.0 * (1.0 + 0.12 * positions)
    weight = base * (scales / math.sqrt(D))[:, None] + 10.0 * lifted[None, :]
    return weight.astype(jnp.bfloat16)


def draw_hidden(key, part):
    lifted = shift_dir(key)
    key = jax.random.fold_in(key, 12)
    total_rows = GROUPS * WINDOW
    flat = jax.random.truncated_normal(key, -5.0, 5.0, (total_rows, D), jnp.float32)
    lift_stride = total_rows // 8
    lift_rows = jnp.array([i * lift_stride + 2 for i in range(8)], jnp.int32)
    lift_sizes = jnp.array([12.0, 20.0, 30.0, 12.0, 20.0, 30.0, 20.0, 30.0], jnp.float32)
    flat = flat.at[lift_rows].add(lift_sizes[:, None] * lifted[None, :])
    return flat.reshape(GROUPS, WINDOW, D).astype(jnp.bfloat16)


def draw_labels(key, part):
    key = jax.random.fold_in(key, 21)
    spots, targets = drawn_spots()
    flat = jax.random.randint(key, (GROUPS * WINDOW,), 0, VOCAB, jnp.int32)
    flat = flat.at[spots].set(targets)
    return flat.reshape(GROUPS, WINDOW)


def draw_loss_mask(key, part):
    key = jax.random.fold_in(key, 22)
    spots, targets = drawn_spots()
    picks = jax.random.randint(key, (GROUPS * WINDOW,), 0, 4, jnp.int32)
    flat = (picks < 3).astype(jnp.int32)
    flat = flat.at[spots].set(1)
    return flat.reshape(GROUPS, WINDOW)


def draw_seq_ids(key, part):
    key = jax.random.fold_in(key, 23)
    delta_key = jax.random.fold_in(key, 1)
    order_key = jax.random.fold_in(key, 2)
    base_len = WINDOW // SEQS
    reach = base_len // 2
    deltas = jax.random.randint(delta_key, (GROUPS, SEQS // 2), -reach, reach + 1, jnp.int32)
    lengths = jnp.concatenate([base_len + deltas, base_len - deltas], axis=1)
    order_keys = jax.random.split(order_key, GROUPS)
    orders = jax.vmap(lambda single: jax.random.permutation(single, SEQS))(order_keys).astype(jnp.int32)
    lengths = jnp.take_along_axis(lengths, orders, axis=1)
    ends = jnp.cumsum(lengths, axis=1).astype(jnp.int32)
    positions = jnp.arange(WINDOW, dtype=jnp.int32)
    passed = (positions[None, :, None] >= ends[:, None, :SEQS - 1]).astype(jnp.int32)
    return jnp.sum(passed, axis=2).astype(jnp.int32)


def draw_old_logp(key, part):
    key = jax.random.fold_in(key, 24)
    values = jax.random.uniform(key, (GROUPS, WINDOW), jnp.float32, -20.0, -13.5)
    return values


def level_of(rng, extent, cuts, low, top_value):
    factor_of = 1.0
    for dim, parts in cuts:
        draws = jax.random.uniform(jax.random.fold_in(jax.random.fold_in(rng, 6), dim), (parts,), jnp.float32, low / len(cuts), top_value / len(cuts))
        factor_of = factor_of * jnp.repeat(jnp.exp(draws), extent[dim] // parts).reshape((-1,) + (1,) * (len(extent) - 1 - dim))
    return factor_of


def scatter_about(stream_key, dims, scale, bound, pieces=(), kind=jnp.bfloat16):
    values = scale * jax.random.normal(stream_key, dims, jnp.float32)
    if pieces:
        values = values * level_of(stream_key, dims, pieces, -0.22, 0.18)
    return jnp.clip(values, -bound, bound).astype(kind)


def setup_inputs(seed: int = 0) -> dict:
    splits = jax.random.split(jax.random.key(seed), 9)
    return {
        "hidden": draw_hidden(jax.random.fold_in(splits[8], 71), 0),
        "head_weight": draw_head_weight(jax.random.fold_in(splits[8], 71), 0),
        "labels": draw_labels(jax.random.fold_in(splits[8], 71), 0),
        "loss_mask": draw_loss_mask(jax.random.fold_in(splits[8], 71), 0),
        "seq_ids": draw_seq_ids(jax.random.fold_in(splits[8], 71), 0),
        "old_logp": draw_old_logp(jax.random.fold_in(splits[8], 71), 0),
        "ref_logp": jnp.clip(-20.0 + 6.5 * jax.random.uniform(splits[6], (GROUPS, WINDOW), jnp.float32) ** level_of(splits[6], (GROUPS, WINDOW), ((0, 4),), -0.2, 0.2), -20.0, -13.5),
        "advantages": scatter_about(splits[7], (GROUPS, SEQS), 1.0, 4.0, ((0, 4),), jnp.float32),
    }


CLIP_LOW = 0.2
CLIP_HIGH = 0.28
DUAL_CLIP = 3.0
KL_COEF = 0.04
KL_CAP = 10.0
LOSS_SCALE = 64.0


def token_weights(logp, targets_mask, seq_row, old_row, ref_row, adv_row):
    seq_match = (seq_row[:, None] == jnp.arange(adv_row.shape[0], dtype=jnp.int32)[None, :]).astype(jnp.float32)
    lengths = jnp.sum(seq_match, axis=0)
    token_adv = jnp.sum(seq_match * adv_row[None, :], axis=1)
    token_len = jnp.sum(seq_match * lengths[None, :], axis=1)
    prob_ratio = jnp.exp(logp - old_row)
    active = jnp.where(token_adv >= 0.0, prob_ratio <= 1.0 + CLIP_HIGH,
                       (prob_ratio >= 1.0 - CLIP_LOW) & (prob_ratio <= DUAL_CLIP))
    policy_term = jnp.where(active, -token_adv * prob_ratio, 0.0)
    log_gap = ref_row - logp
    exp_gap = jnp.exp(log_gap)
    kl_value = exp_gap - log_gap - 1.0
    penalty = jnp.where(kl_value < KL_CAP, 1.0 - exp_gap, 0.0)
    return LOSS_SCALE * targets_mask.astype(jnp.float32) * (policy_term + KL_COEF * penalty) / token_len


def reference(hidden, head_weight, labels, loss_mask, seq_ids, old_logp, ref_logp, advantages):
    entries = head_weight.shape[0]

    def per_group(inputs):
        states, targets, masks, seq_row, old_row, ref_row, adv_row = inputs
        logits = jnp.dot(states, head_weight.T, preferred_element_type=jnp.float32)
        row_max = jnp.max(logits, axis=1)
        row_sum = jnp.sum(jnp.exp(logits - row_max[:, None]), axis=1)
        log_total = row_max + jnp.log(row_sum)
        label_logit = jnp.take_along_axis(logits, targets[:, None].astype(jnp.int32), axis=1)[:, 0]
        token_grad = token_weights(label_logit - log_total, masks, seq_row, old_row, ref_row, adv_row)
        one_hot = (targets[:, None] == jnp.arange(entries, dtype=jnp.int32)[None, :]).astype(jnp.float32)
        likely = jnp.exp(logits - log_total[:, None])
        grad_logits = (token_grad[:, None] * (one_hot - likely)).astype(jnp.bfloat16)
        state_grad = jnp.dot(grad_logits, head_weight, preferred_element_type=jnp.float32).astype(jnp.bfloat16)
        return grad_logits, state_grad

    grad_all, hidden_grad = lax.map(per_group, (hidden, labels, loss_mask, seq_ids, old_logp, ref_logp, advantages))
    flat_grads = grad_all.reshape(-1, entries)
    flat_states = hidden.reshape(-1, hidden.shape[2])
    head_grad = jnp.dot(flat_grads.T, flat_states, preferred_element_type=jnp.float32).astype(jnp.bfloat16)
    return hidden_grad, head_grad
```

```python
import functools

import jax
import jax.numpy as jnp
from jax import lax
from jax.experimental import pallas as pl
from jax.experimental.pallas import tpu as pltpu
from jax.sharding import PartitionSpec as P

CLIP_LOW = 0.2
CLIP_HIGH = 0.28
DUAL_CLIP = 3.0
KL_COEF = 0.04
KL_CAP = 10.0
LOSS_SCALE = 64.0

MESH = pl.DeviceIdType.MESH
F32 = jnp.float32
BF16 = jnp.bfloat16

NX = 4
NC = 4
NH = 2
NY = NC * NH
NZ = 8
WIN = 256
TOK = WIN // NC
HALF = TOK // 2
QTR = HALF // 2
D = 2048
ROWS = 896
CH = 128
COLS = D // NX
PART = 512
NPART = D // PART
SPLIT = ROWS // 2


def token_weights(logp, mask, seq, old, ref, adv_ref):
    adv = jnp.zeros_like(logp)
    length = jnp.zeros_like(logp)
    for s in range(adv_ref.shape[1]):
        match = (seq == s).astype(F32)
        count = jnp.sum(match, axis=1, keepdims=True)
        adv = adv + match * adv_ref[0:1, s : s + 1]
        length = length + match * count
    ratio = jnp.exp(logp - old)
    low = jnp.where(ratio >= 1.0 - CLIP_LOW, jnp.where(ratio <= DUAL_CLIP, 1.0, 0.0), 0.0)
    active = jnp.where(adv >= 0.0, jnp.where(ratio <= 1.0 + CLIP_HIGH, 1.0, 0.0), low)
    policy = jnp.where(active > 0.0, -adv * ratio, 0.0)
    gap = ref - logp
    exp_gap = jnp.exp(gap)
    penalty = jnp.where(exp_gap - gap - 1.0 < KL_CAP, 1.0 - exp_gap, 0.0)
    return LOSS_SCALE * mask.astype(F32) * (policy + KL_COEF * penalty) / length


def merge(ref, n):
    top = ref[0, 0:2, :]
    for i in range(1, n):
        top = jnp.maximum(top, ref[i, 0:2, :])
    total = jnp.zeros_like(top)
    label = jnp.zeros_like(top)
    for i in range(n):
        total = total + ref[i, 2:4, :] * jnp.exp(ref[i, 0:2, :] - top)
        label = label + ref[i, 4:6, :]
    return top, total, label


def put(ref, slot, top, total, label):
    ref[slot] = jnp.concatenate([top, total, label, jnp.zeros_like(top)], axis=0)


def fold(row):
    return jnp.concatenate([row[:, :128], row[:, 128:]], axis=0)


def unfold(tile):
    return jnp.concatenate([tile[0:1, :], tile[1:2, :]], axis=1)


def kernel(
    hid_ref,
    w_hbm,
    lab_ref,
    mask_ref,
    seq_ref,
    old_ref,
    refp_ref,
    adv_ref,
    hg_ref,
    head_hbm,
    w,
    win,
    hc,
    logit,
    q,
    gt,
    g,
    keep,
    e1s,
    e1r,
    rsa,
    rsb,
    ra1,
    rb1,
    ra2s,
    rb2s,
    ra2,
    rb2,
    fin,
    st0,
    st1,
    st2,
    scale,
    acc,
    head,
    loc_sem,
    a_send,
    a_recv,
    f_send,
    f_recv,
    h_send,
    h_recv,
    hf_send,
    hf_recv,
    q_send,
    q_recv,
    c0_send,
    c0_recv,
    c1_send,
    c1_recv,
    c2_send,
    c2_recv,
    x_send,
    x_recv,
    e_send,
    e_recv,
    ra1_send,
    ra1_recv,
    rb1_send,
    rb1_recv,
    ra2_send,
    ra2_recv,
    rb2_send,
    rb2_recv,
    fin_send,
    fin_recv,
):
    x = lax.axis_index("dp")
    c = lax.axis_index("ctx")
    v = lax.axis_index("vocab")
    h = v // (NZ * 2)
    z = (v // 2) % NZ
    k = v % 2
    y = h * NC + c

    def at_y(to):
        return (x, to % NC, (to // NC) * (NZ * 2) + z * 2 + k)

    def at_z(to):
        return (x, c, h * (NZ * 2) + to * 2 + k)

    def at_x(to):
        return (to, c, v)

    partner = (x, c, h * (NZ * 2) + z * 2 + (1 - k))

    def send(src, dst, ssem, rsem, to):
        copy = pltpu.make_async_remote_copy(
            src_ref=src, dst_ref=dst, send_sem=ssem, recv_sem=rsem, device_id=to, device_id_type=MESH
        )
        copy.start()
        return copy

    def arrived(dst, ssem, rsem, to):
        pltpu.make_async_remote_copy(
            src_ref=dst, dst_ref=dst, send_sem=ssem, recv_sem=rsem, device_id=to, device_id_type=MESH
        ).wait_recv()

    sent = []

    load_w = pltpu.make_async_copy(w_hbm, w, loc_sem.at[0])
    load_w.start()

    barrier = pltpu.get_barrier_semaphore()
    peers = [partner]
    peers += [at_y((y + d) % NY) for d in range(1, NY)]
    peers += [at_z((z + d) % NZ) for d in range(1, NZ)]
    peers += [at_x((x + d) % NX) for d in range(1, NX)]
    for peer in peers:
        pl.semaphore_signal(barrier, inc=1, device_id=peer, device_id_type=MESH)
    win[pl.ds(pl.multiple_of(c * TOK, TOK), TOK), :] = hid_ref[0]
    pl.semaphore_wait(barrier, len(peers))

    def half_block(block, half):
        return win.at[pl.ds(pl.multiple_of(block * TOK + half * HALF, HALF), HALF), :]

    mine = half_block(c, k)
    far = (y + NY + 2 - 4 * k) % NY
    for i, to in enumerate(((y + 1) % NY, (y + NY - 1) % NY, far)):
        sent.append(send(mine, mine, a_send.at[i], a_recv.at[i], at_y(to)))
    from_block = ((c + NC - 1) % NC, (c + 1) % NC, (c + 2) % NC)
    for i in range(3):
        piece = half_block(from_block[i], k)
        arrived(piece, a_send.at[i], a_recv.at[i], partner)
        sent.append(send(piece, piece, f_send.at[i], f_recv.at[i], partner))
    for i in range(3):
        piece = half_block(from_block[i], 1 - k)
        arrived(piece, f_send.at[i], f_recv.at[i], partner)

    half_win = pl.ds(pl.multiple_of(k * (WIN // 2), WIN // 2), WIN // 2)
    other_win = pl.ds(pl.multiple_of((1 - k) * (WIN // 2), WIN // 2), WIN // 2)
    place = {0: 0, 1: 1, 3: 2, 2: 3}
    for d in (1, 3, 2):
        to = (x + d) % NX
        src = win.at[half_win, pl.ds(pl.multiple_of(to * COLS, COLS), COLS)]
        dst = hc.at[place[d], half_win, :]
        sent.append(send(src, dst, h_send.at[d - 1], h_recv.at[d - 1], at_x(to)))

    load_w.wait()
    logit[...] = lax.dot_general(
        w[...], win[...], (((1,), (1,)), ((), ())), preferred_element_type=F32
    )
    base = (c * (NH * NZ * 2) + v) * ROWS
    local_label = lab_ref[...] - base

    def hit(i):
        rows = lax.broadcasted_iota(jnp.int32, (CH, WIN), 0) + i * CH
        return rows == local_label

    def rows_of(i):
        return pl.ds(pl.multiple_of(i * CH, CH), CH)

    def stat_step(i, carry):
        top, label = carry
        part = logit[rows_of(i), :]
        top = jnp.maximum(top, jnp.max(part, axis=0, keepdims=True))
        label = label + jnp.sum(jnp.where(hit(i), part, 0.0), axis=0, keepdims=True)
        return top, label

    top, label = lax.fori_loop(
        0, ROWS // CH, stat_step, (jnp.full((1, WIN), -jnp.inf, F32), jnp.zeros((1, WIN), F32))
    )

    def exp_step(i, total):
        part = jnp.exp(logit[rows_of(i), :] - top)
        q[0, rows_of(i), :] = jnp.where(hit(i), -1.0, part).astype(BF16)
        return total + jnp.sum(part, axis=0, keepdims=True)

    total = lax.fori_loop(0, ROWS // CH, exp_step, jnp.zeros((1, WIN), F32))

    put(st0, k, fold(top), fold(total), fold(label))
    sent.append(send(st0.at[k], st0.at[k], c0_send, c0_recv, partner))

    right, left = (x + 1) % NX, (x + NX - 1) % NX
    lo, hi = pl.ds(0, SPLIT), pl.ds(SPLIT, SPLIT)
    sent.append(send(q.at[0, lo, :], q.at[1, lo, :], q_send.at[0], q_recv.at[0], at_x(right)))
    sent.append(send(q.at[0, hi, :], q.at[2, hi, :], q_send.at[1], q_recv.at[1], at_x(left)))
    sent.append(send(q.at[0, hi, :], q.at[1, hi, :], q_send.at[2], q_recv.at[2], at_x(right)))
    sent.append(send(q.at[0, lo, :], q.at[2, lo, :], q_send.at[3], q_recv.at[3], at_x(left)))

    arrived(st0.at[1 - k], c0_send, c0_recv, partner)
    put(st1, y, *merge(st0, 2))
    for d in range(1, NY):
        to = (y + d) % NY
        sent.append(send(st1.at[y], st1.at[y], c1_send.at[d - 1], c1_recv.at[d - 1], at_y(to)))
    for d in range(1, NY):
        arrived(st1.at[(y + NY - d) % NY], c1_send.at[d - 1], c1_recv.at[d - 1], partner)
    put(st2, z, *merge(st1, NY))
    for d in range(1, NZ):
        to = (z + d) % NZ
        sent.append(send(st2.at[z], st2.at[z], c2_send.at[d - 1], c2_recv.at[d - 1], at_z(to)))
    for d in range(1, NZ):
        arrived(st2.at[(z + NZ - d) % NZ], c2_send.at[d - 1], c2_recv.at[d - 1], partner)
    all_top, all_total, all_label = merge(st2, NZ)
    log_total = unfold(all_top + jnp.log(all_total))
    logp = unfold(all_label) - log_total
    coeff = token_weights(
        logp, mask_ref[...], seq_ref[...], old_ref[...], refp_ref[...], adv_ref
    )

    factor = coeff * jnp.exp(top - log_total)
    label_grad = coeff * (1.0 - jnp.exp(logp))
    put(scale, 0, fold(factor), fold(label_grad), fold(label_grad))
    for d in (1, 3, 2):
        sent.append(
            send(scale.at[0], scale.at[d], x_send.at[d - 1], x_recv.at[d - 1], at_x((x + d) % NX))
        )

    def grad_step(i, carry):
        grad = coeff * (hit(i).astype(F32) - jnp.exp(logit[rows_of(i), :] - log_total))
        gt[rows_of(i), 0:WIN] = grad.astype(BF16)
        turned = grad.T.astype(BF16)
        for j in range(NC):
            for half in range(2):
                row = j * HALF + (WIN // 2) * (k if half else 1 - k)
                start = j * TOK + half * HALF
                g[pl.ds(pl.multiple_of(row, HALF), HALF), rows_of(i)] = turned[start : start + HALF]
        return carry

    lax.fori_loop(0, ROWS // CH, grad_step, 0)

    for n in range(NPART):
        cols = pl.ds(n * PART, PART)
        value = jnp.dot(g[...], w[:, n * PART : (n + 1) * PART], preferred_element_type=F32)
        e1s[:, cols] = value[: WIN // 2].astype(BF16)
        keep[:, cols] = value[WIN // 2 :]
        sent.append(send(e1s.at[:, cols], e1r.at[:, cols], e_send.at[n], e_recv.at[n], partner))

    arrived(q.at[1, lo, :], q_send.at[0], q_recv.at[0], partner)
    sent.append(send(q.at[1, lo, :], q.at[3, lo, :], q_send.at[4], q_recv.at[4], at_x(right)))
    arrived(q.at[2, hi, :], q_send.at[1], q_recv.at[1], partner)
    sent.append(send(q.at[2, hi, :], q.at[3, hi, :], q_send.at[5], q_recv.at[5], at_x(left)))

    for n in range(NPART):
        cols = pl.ds(n * PART, PART)
        arrived(e1r.at[:, cols], e_send.at[n], e_recv.at[n], partner)
        for j in range(NC):
            rows = slice(j * HALF, (j + 1) * HALF)
            both = keep[rows, n * PART : (n + 1) * PART] + e1r[rows, n * PART : (n + 1) * PART].astype(F32)
            both = both.astype(BF16)
            rsa[j, :, cols] = both[:QTR]
            for m in range(PART // 128):
                block = n * (PART // 128) + m
                hh, zz = block // NZ, block % NZ
                rsb[zz, hh * TOK + j * QTR : hh * TOK + (j + 1) * QTR, :] = both[
                    QTR:, m * 128 : (m + 1) * 128
                ]

    for d in range(1, NY):
        to = (y + d) % NY
        src = rsa.at[to % NC, :, pl.ds(pl.multiple_of((to // NC) * (D // NH), D // NH), D // NH)]
        sent.append(send(src, ra1.at[d], ra1_send.at[d - 1], ra1_recv.at[d - 1], at_y(to)))
        to = (z + d) % NZ
        sent.append(send(rsb.at[to], rb1.at[d], rb1_send.at[d - 1], rb1_recv.at[d - 1], at_z(to)))

    for d in (1, 3, 2):
        piece = hc.at[place[d], half_win, :]
        arrived(piece, h_send.at[d - 1], h_recv.at[d - 1], partner)
        sent.append(send(piece, piece, hf_send.at[d - 1], hf_recv.at[d - 1], partner))
    hc[0] = win[:, pl.ds(pl.multiple_of(x * COLS, COLS), COLS)]

    def form(slot, first, last, factor_row, label_row):
        def step(i, carry):
            rows = pl.ds(pl.multiple_of(i * 64, 64), 64)
            part = q[slot, rows, :].astype(F32)
            grad = jnp.where(part < 0.0, label_row, -part * factor_row)
            gt[rows, slot * WIN : (slot + 1) * WIN] = grad.astype(BF16)
            return carry

        lax.fori_loop(first // 64, last // 64, step, 0)

    def rows_for(d):
        arrived(scale.at[d], x_send.at[d - 1], x_recv.at[d - 1], partner)
        return unfold(scale[d, 0:2, :]), unfold(scale[d, 2:4, :])

    own = rsa[c, :, pl.ds(pl.multiple_of(h * (D // NH), D // NH), D // NH)].astype(F32)
    for d in range(1, NY):
        arrived(ra1.at[d], ra1_send.at[d - 1], ra1_recv.at[d - 1], partner)
        own = own + ra1[d].astype(F32)
    ra2s[...] = own.astype(BF16)
    for d in range(1, NZ):
        to = (z + d) % NZ
        src = ra2s.at[:, pl.ds(pl.multiple_of(to * 128, 128), 128)]
        sent.append(send(src, ra2.at[d], ra2_send.at[d - 1], ra2_recv.at[d - 1], at_z(to)))
    own = rsb[z].astype(F32)
    for d in range(1, NZ):
        arrived(rb1.at[d], rb1_send.at[d - 1], rb1_recv.at[d - 1], partner)
        own = own + rb1[d].astype(F32)
    rb2s[...] = own.astype(BF16)
    for d in range(1, NY):
        to = (y + d) % NY
        src = rb2s.at[pl.ds(pl.multiple_of((to // NC) * TOK + (to % NC) * QTR, QTR), QTR), :]
        sent.append(send(src, rb2.at[d], rb2_send.at[d - 1], rb2_recv.at[d - 1], at_y(to)))

    for d in (1, 3, 2):
        piece = hc.at[place[d], other_win, :]
        arrived(piece, hf_send.at[d - 1], hf_recv.at[d - 1], partner)
    near = rows_for(1)
    arrived(q.at[1, hi, :], q_send.at[2], q_recv.at[2], partner)
    form(1, 0, ROWS, *near)
    near = rows_for(3)
    arrived(q.at[2, lo, :], q_send.at[3], q_recv.at[3], partner)
    form(2, 0, ROWS, *near)
    acc[...] = jnp.dot(
        gt[:, : 3 * WIN], hc[0:3].reshape(3 * WIN, COLS), preferred_element_type=F32
    )

    own = ra2s[:, pl.ds(pl.multiple_of(z * 128, 128), 128)].astype(F32)
    for d in range(1, NZ):
        arrived(ra2.at[d], ra2_send.at[d - 1], ra2_recv.at[d - 1], partner)
        own = own + ra2[d].astype(F32)
    fin[0, 0:QTR, :] = own.astype(BF16)
    own = rb2s[pl.ds(pl.multiple_of(h * TOK + c * QTR, QTR), QTR), :].astype(F32)
    for d in range(1, NY):
        arrived(rb2.at[d], rb2_send.at[d - 1], rb2_recv.at[d - 1], partner)
        own = own + rb2[d].astype(F32)
    fin[0, QTR:HALF, :] = own.astype(BF16)
    sent.append(send(fin.at[0], fin.at[1], fin_send, fin_recv, partner))

    across = rows_for(2)
    arrived(q.at[3, lo, :], q_send.at[4], q_recv.at[4], partner)
    arrived(q.at[3, hi, :], q_send.at[5], q_recv.at[5], partner)
    form(3, 0, ROWS, *across)
    head[...] = (
        acc[...] + jnp.dot(gt[:, 3 * WIN :], hc[3], preferred_element_type=F32)
    ).astype(BF16)
    store = pltpu.make_async_copy(head, head_hbm, loc_sem.at[1])
    store.start()

    arrived(fin.at[1], fin_send, fin_recv, partner)
    for slot, row in ((0, k), (1, 1 - k)):
        value = fin[slot].astype(F32)
        value = jnp.where(k == 0, value[:, :64], value[:, 64:])
        hg_ref[0, pl.ds(pl.multiple_of(row * HALF, HALF), HALF), :] = value.astype(BF16)
    store.wait()
    for copy in sent:
        copy.wait_send()


def body(*args):
    vmem = pl.BlockSpec(memory_space=pltpu.VMEM)
    hbm = pl.BlockSpec(memory_space=pl.ANY)
    dma = pltpu.SemaphoreType.DMA
    return pl.pallas_call(
        kernel,
        out_shape=(
            jax.ShapeDtypeStruct((1, TOK, D // (NH * NZ * 2)), BF16),
            jax.ShapeDtypeStruct((ROWS, COLS), BF16),
        ),
        in_specs=[vmem, hbm] + [vmem] * 6,
        out_specs=(vmem, hbm),
        scratch_shapes=[
            pltpu.VMEM((ROWS, D), BF16),
            pltpu.VMEM((WIN, D), BF16),
            pltpu.VMEM((NX, WIN, COLS), BF16),
            pltpu.VMEM((ROWS, WIN), F32),
            pltpu.VMEM((NX, ROWS, WIN), BF16),
            pltpu.VMEM((ROWS, NX * WIN), BF16),
            pltpu.VMEM((WIN, ROWS), BF16),
            pltpu.VMEM((WIN // 2, D), F32),
            pltpu.VMEM((WIN // 2, D), BF16),
            pltpu.VMEM((WIN // 2, D), BF16),
            pltpu.VMEM((NC, QTR, D), BF16),
            pltpu.VMEM((NZ, NH * TOK, 128), BF16),
            pltpu.VMEM((NY, QTR, D // NH), BF16),
            pltpu.VMEM((NZ, NH * TOK, 128), BF16),
            pltpu.VMEM((QTR, D // NH), BF16),
            pltpu.VMEM((NH * TOK, 128), BF16),
            pltpu.VMEM((NZ, QTR, 128), BF16),
            pltpu.VMEM((NY, QTR, 128), BF16),
            pltpu.VMEM((2, HALF, 128), BF16),
            pltpu.VMEM((2, 8, 128), F32),
            pltpu.VMEM((NY, 8, 128), F32),
            pltpu.VMEM((NZ, 8, 128), F32),
            pltpu.VMEM((NX, 8, 128), F32),
            pltpu.VMEM((ROWS, COLS), F32),
            pltpu.VMEM((ROWS, COLS), BF16),
            dma((2,)),
            dma((3,)),
            dma((3,)),
            dma((3,)),
            dma((3,)),
            dma((3,)),
            dma((3,)),
            dma((3,)),
            dma((3,)),
            dma((6,)),
            dma((6,)),
            dma,
            dma,
            dma((NY - 1,)),
            dma((NY - 1,)),
            dma((NZ - 1,)),
            dma((NZ - 1,)),
            dma((NX - 1,)),
            dma((NX - 1,)),
            dma((NPART,)),
            dma((NPART,)),
            dma((NY - 1,)),
            dma((NY - 1,)),
            dma((NZ - 1,)),
            dma((NZ - 1,)),
            dma((NZ - 1,)),
            dma((NZ - 1,)),
            dma((NY - 1,)),
            dma((NY - 1,)),
            dma,
            dma,
        ],
        compiler_params=pltpu.CompilerParams(
            collective_id=0, has_side_effects=True, vmem_limit_bytes=48 * 1024 * 1024
        ),
        cost_estimate=pl.CostEstimate(
            flops=6 * WIN * D * ROWS, bytes_accessed=2 * ROWS * (D + COLS), transcendentals=4 * ROWS * WIN
        ),
    )(*args)


def solution(mesh):
    placed = (P("dp", "ctx", None), P(("ctx", "vocab"), None)) + (P("dp", None),) * 6
    return jax.shard_map(
        body,
        mesh=mesh,
        in_specs=placed,
        out_specs=(P("dp", "ctx", "vocab"), P(("ctx", "vocab"), "dp")),
        check_vma=False,
    )
```

```python
import functools

import jax
import jax.numpy as jnp
from jax import lax
from jax.experimental import pallas as pl
from jax.experimental.pallas import tpu as pltpu
from jax.sharding import PartitionSpec as P

CLIP_LOW = 0.2
CLIP_HIGH = 0.28
DUAL_CLIP = 3.0
KL_COEF = 0.04
KL_CAP = 10.0
LOSS_SCALE = 64.0

MESH = pl.DeviceIdType.MESH
F32 = jnp.float32
BF16 = jnp.bfloat16

NX = 4
NC = 4
NH = 2
NY = NC * NH
NZ = 8
WIN = 256
TOK = WIN // NC
HALF = TOK // 2
QTR = HALF // 2
D = 2048
ROWS = 896
CH = 128
COLS = D // NX
PART = 512
NPART = D // PART
SPLIT = ROWS // 2


def token_weights(logp, mask, seq, old, ref, adv_ref):
    adv = jnp.zeros_like(logp)
    length = jnp.zeros_like(logp)
    for s in range(adv_ref.shape[1]):
        match = (seq == s).astype(F32)
        count = jnp.sum(match, axis=1, keepdims=True)
        adv = adv + match * adv_ref[0:1, s : s + 1]
        length = length + match * count
    ratio = jnp.exp(logp - old)
    low = jnp.where(ratio >= 1.0 - CLIP_LOW, jnp.where(ratio <= DUAL_CLIP, 1.0, 0.0), 0.0)
    active = jnp.where(adv >= 0.0, jnp.where(ratio <= 1.0 + CLIP_HIGH, 1.0, 0.0), low)
    policy = jnp.where(active > 0.0, -adv * ratio, 0.0)
    gap = ref - logp
    exp_gap = jnp.exp(gap)
    penalty = jnp.where(exp_gap - gap - 1.0 < KL_CAP, 1.0 - exp_gap, 0.0)
    return LOSS_SCALE * mask.astype(F32) * (policy + KL_COEF * penalty) / length


def merge(ref, n):
    top = ref[0, 0:2, :]
    for i in range(1, n):
        top = jnp.maximum(top, ref[i, 0:2, :])
    total = jnp.zeros_like(top)
    label = jnp.zeros_like(top)
    for i in range(n):
        total = total + ref[i, 2:4, :] * jnp.exp(ref[i, 0:2, :] - top)
        label = label + ref[i, 4:6, :]
    return top, total, label


def put(ref, slot, top, total, label):
    ref[slot] = jnp.concatenate([top, total, label, jnp.zeros_like(top)], axis=0)


def fold(row):
    return jnp.concatenate([row[:, :128], row[:, 128:]], axis=0)


def unfold(tile):
    return jnp.concatenate([tile[0:1, :], tile[1:2, :]], axis=1)


SEMS = 80


def kernel(
    hid_hbm,
    w_hbm,
    lab_hbm,
    mask_hbm,
    seq_hbm,
    old_hbm,
    refp_hbm,
    adv_hbm,
    hg_ref,
    head_ref,
    w,
    win,
    hc,
    logit,
    q,
    gt,
    g,
    keep,
    e1s,
    e1r,
    rsa,
    rsb,
    ra1,
    rb1,
    ra2s,
    rb2s,
    ra2,
    rb2,
    fin,
    st0,
    st1,
    st2,
    scale,
    acc,
    lab_ref,
    mask_ref,
    seq_ref,
    old_ref,
    refp_ref,
    adv_ref,
    loc_sem,
    send_sems,
    recv_sems,
):
    x = lax.axis_index("dp")
    c = lax.axis_index("ctx")
    v = lax.axis_index("vocab")
    h = v // (NZ * 2)
    z = (v // 2) % NZ
    k = v % 2
    y = h * NC + c

    def at_y(to):
        return (x, to % NC, (to // NC) * (NZ * 2) + z * 2 + k)

    def at_z(to):
        return (x, c, h * (NZ * 2) + to * 2 + k)

    def at_x(to):
        return (to, c, v)

    partner = (x, c, h * (NZ * 2) + z * 2 + (1 - k))

    sent = []
    coming = {}

    def send(name, src, dst, landing, to):
        at = len(sent)
        copy = pltpu.make_async_remote_copy(
            src_ref=src,
            dst_ref=dst,
            send_sem=send_sems.at[at],
            recv_sem=recv_sems.at[at],
            device_id=to,
            device_id_type=MESH,
        )
        copy.start()
        sent.append(copy)
        coming[name] = pltpu.make_async_remote_copy(
            src_ref=landing,
            dst_ref=landing,
            send_sem=send_sems.at[at],
            recv_sem=recv_sems.at[at],
            device_id=to,
            device_id_type=MESH,
        )

    def arrived(name):
        coming.pop(name).wait_recv()

    def drain():
        for name in list(coming):
            arrived(name)
        for copy in sent:
            copy.wait_send()

    block = pl.ds(pl.multiple_of(c * TOK, TOK), TOK)
    load_hid = pltpu.make_async_copy(hid_hbm.at[0], win.at[block, :], loc_sem.at[0])
    load_hid.start()
    load_w = pltpu.make_async_copy(w_hbm, w, loc_sem.at[1])
    load_w.start()
    loads = []
    for i, (src, dst) in enumerate(
        (
            (lab_hbm, lab_ref),
            (mask_hbm, mask_ref),
            (seq_hbm, seq_ref),
            (old_hbm, old_ref),
            (refp_hbm, refp_ref),
            (adv_hbm, adv_ref),
        )
    ):
        loads.append(pltpu.make_async_copy(src, dst, loc_sem.at[2 + i]))
        loads[-1].start()

    barrier = pltpu.get_barrier_semaphore()
    peers = [partner]
    peers += [at_y((y + d) % NY) for d in range(1, NY)]
    peers += [at_z((z + d) % NZ) for d in range(1, NZ)]
    peers += [at_x((x + d) % NX) for d in range(1, NX)]
    for peer in peers:
        pl.semaphore_signal(barrier, inc=1, device_id=peer, device_id_type=MESH)
    pl.semaphore_wait(barrier, len(peers))

    def half_block(number, half):
        return win.at[pl.ds(pl.multiple_of(number * TOK + half * HALF, HALF), HALF), :]

    far = (y + NY + 2 - 4 * k) % NY
    from_block = ((c + NC - 1) % NC, (c + 1) % NC, (c + 2) % NC)
    mine = hid_hbm.at[0, pl.ds(pl.multiple_of(k * HALF, HALF), HALF), :]
    for i, to in enumerate(((y + 1) % NY, (y + NY - 1) % NY, far)):
        send(f"a{i}", mine, half_block(c, k), half_block(from_block[i], k), at_y(to))
    for i in range(3):
        arrived(f"a{i}")
        piece = half_block(from_block[i], k)
        send(f"f{i}", piece, piece, half_block(from_block[i], 1 - k), partner)
    load_hid.wait()
    for i in range(3):
        arrived(f"f{i}")

    half_win = pl.ds(pl.multiple_of(k * (WIN // 2), WIN // 2), WIN // 2)
    other_win = pl.ds(pl.multiple_of((1 - k) * (WIN // 2), WIN // 2), WIN // 2)
    place = {0: 0, 1: 1, 3: 2, 2: 3}
    for d in (1, 3, 2):
        to = (x + d) % NX
        src = win.at[half_win, pl.ds(pl.multiple_of(to * COLS, COLS), COLS)]
        dst = hc.at[place[d], half_win, :]
        send(f"h{d}", src, dst, dst, at_x(to))

    load_w.wait()
    for load in loads:
        load.wait()
    logit[...] = lax.dot_general(
        w[...], win[...], (((1,), (1,)), ((), ())), preferred_element_type=F32
    )
    base = (c * (NH * NZ * 2) + v) * ROWS
    local_label = lab_ref[...] - base

    def hit(i):
        rows = lax.broadcasted_iota(jnp.int32, (CH, WIN), 0) + i * CH
        return rows == local_label

    def rows_of(i):
        return pl.ds(pl.multiple_of(i * CH, CH), CH)

    def stat_step(i, carry):
        top, label = carry
        part = logit[rows_of(i), :]
        top = jnp.maximum(top, jnp.max(part, axis=0, keepdims=True))
        label = label + jnp.sum(jnp.where(hit(i), part, 0.0), axis=0, keepdims=True)
        return top, label

    top, label = lax.fori_loop(
        0, ROWS // CH, stat_step, (jnp.full((1, WIN), -jnp.inf, F32), jnp.zeros((1, WIN), F32))
    )

    def exp_step(i, total):
        part = jnp.exp(logit[rows_of(i), :] - top)
        q[0, rows_of(i), :] = jnp.where(hit(i), -1.0, part).astype(BF16)
        return total + jnp.sum(part, axis=0, keepdims=True)

    total = lax.fori_loop(0, ROWS // CH, exp_step, jnp.zeros((1, WIN), F32))

    put(st0, k, fold(top), fold(total), fold(label))
    send("c", st0.at[k], st0.at[k], st0.at[1 - k], partner)

    right, left = (x + 1) % NX, (x + NX - 1) % NX
    lo, hi = pl.ds(0, SPLIT), pl.ds(SPLIT, SPLIT)
    send("q1lo", q.at[0, lo, :], q.at[1, lo, :], q.at[1, lo, :], at_x(right))
    send("q2hi", q.at[0, hi, :], q.at[2, hi, :], q.at[2, hi, :], at_x(left))
    send("q1hi", q.at[0, hi, :], q.at[1, hi, :], q.at[1, hi, :], at_x(right))
    send("q2lo", q.at[0, lo, :], q.at[2, lo, :], q.at[2, lo, :], at_x(left))
    arrived("c")
    put(st1, y, *merge(st0, 2))
    for d in range(1, NY):
        send(f"cy{d}", st1.at[y], st1.at[y], st1.at[(y + NY - d) % NY], at_y((y + d) % NY))
    for d in range(1, NY):
        arrived(f"cy{d}")
    put(st2, z, *merge(st1, NY))
    for d in range(1, NZ):
        send(f"cz{d}", st2.at[z], st2.at[z], st2.at[(z + NZ - d) % NZ], at_z((z + d) % NZ))
    for d in range(1, NZ):
        arrived(f"cz{d}")
    all_top, all_total, all_label = merge(st2, NZ)
    log_total = unfold(all_top + jnp.log(all_total))
    logp = unfold(all_label) - log_total
    coeff = token_weights(
        logp, mask_ref[...], seq_ref[...], old_ref[...], refp_ref[...], adv_ref
    )

    factor = coeff * jnp.exp(top - log_total)
    label_grad = coeff * (1.0 - jnp.exp(logp))
    put(scale, 0, fold(factor), fold(label_grad), fold(label_grad))
    for d in (1, 3, 2):
        send(f"x{d}", scale.at[0], scale.at[d], scale.at[d], at_x((x + d) % NX))

    def grad_step(i, carry):
        grad = coeff * (hit(i).astype(F32) - jnp.exp(logit[rows_of(i), :] - log_total))
        gt[rows_of(i), 0:WIN] = grad.astype(BF16)
        turned = grad.T.astype(BF16)
        for j in range(NC):
            for half in range(2):
                row = j * HALF + (WIN // 2) * (k if half else 1 - k)
                start = j * TOK + half * HALF
                g[pl.ds(pl.multiple_of(row, HALF), HALF), rows_of(i)] = turned[start : start + HALF]
        return carry

    lax.fori_loop(0, ROWS // CH, grad_step, 0)

    for n in range(NPART):
        cols = pl.ds(n * PART, PART)
        value = jnp.dot(g[...], w[:, n * PART : (n + 1) * PART], preferred_element_type=F32)
        e1s[:, cols] = value[: WIN // 2].astype(BF16)
        keep[:, cols] = value[WIN // 2 :]
        send(f"e{n}", e1s.at[:, cols], e1r.at[:, cols], e1r.at[:, cols], partner)
    arrived("q1lo")
    send("q3lo", q.at[1, lo, :], q.at[3, lo, :], q.at[3, lo, :], at_x(right))
    arrived("q2hi")
    send("q3hi", q.at[2, hi, :], q.at[3, hi, :], q.at[3, hi, :], at_x(left))

    for n in range(NPART):
        cols = pl.ds(n * PART, PART)
        arrived(f"e{n}")
        for j in range(NC):
            rows = slice(j * HALF, (j + 1) * HALF)
            both = keep[rows, n * PART : (n + 1) * PART] + e1r[rows, n * PART : (n + 1) * PART].astype(F32)
            both = both.astype(BF16)
            rsa[j, :, cols] = both[:QTR]
            for m in range(PART // 128):
                block = n * (PART // 128) + m
                hh, zz = block // NZ, block % NZ
                rsb[zz, hh * TOK + j * QTR : hh * TOK + (j + 1) * QTR, :] = both[
                    QTR:, m * 128 : (m + 1) * 128
                ]

    for d in range(1, NY):
        to = (y + d) % NY
        src = rsa.at[to % NC, :, pl.ds(pl.multiple_of((to // NC) * (D // NH), D // NH), D // NH)]
        send(f"ya{d}", src, ra1.at[d], ra1.at[d], at_y(to))
        to = (z + d) % NZ
        send(f"zb{d}", rsb.at[to], rb1.at[d], rb1.at[d], at_z(to))

    for d in (1, 3, 2):
        arrived(f"h{d}")
        piece = hc.at[place[d], half_win, :]
        send(f"g{d}", piece, piece, hc.at[place[d], other_win, :], partner)
    hc[0] = win[:, pl.ds(pl.multiple_of(x * COLS, COLS), COLS)]

    def form(slot, first, last, factor_row, label_row):
        def step(i, carry):
            rows = pl.ds(pl.multiple_of(i * 64, 64), 64)
            part = q[slot, rows, :].astype(F32)
            grad = jnp.where(part < 0.0, label_row, -part * factor_row)
            gt[rows, slot * WIN : (slot + 1) * WIN] = grad.astype(BF16)
            return carry

        lax.fori_loop(first // 64, last // 64, step, 0)

    def rows_for(d):
        arrived(f"x{d}")
        return unfold(scale[d, 0:2, :]), unfold(scale[d, 2:4, :])

    own = rsa[c, :, pl.ds(pl.multiple_of(h * (D // NH), D // NH), D // NH)].astype(F32)
    for d in range(1, NY):
        arrived(f"ya{d}")
        own = own + ra1[d].astype(F32)
    ra2s[...] = own
    for d in range(1, NZ):
        to = (z + d) % NZ
        src = ra2s.at[:, pl.ds(pl.multiple_of(to * 128, 128), 128)]
        send(f"za{d}", src, ra2.at[d], ra2.at[d], at_z(to))
    own = rsb[z].astype(F32)
    for d in range(1, NZ):
        arrived(f"zb{d}")
        own = own + rb1[d].astype(F32)
    rb2s[...] = own
    for d in range(1, NY):
        to = (y + d) % NY
        src = rb2s.at[pl.ds(pl.multiple_of((to // NC) * TOK + (to % NC) * QTR, QTR), QTR), :]
        send(f"yb{d}", src, rb2.at[d], rb2.at[d], at_y(to))
    for d in (1, 3, 2):
        arrived(f"g{d}")
    near = rows_for(1)
    arrived("q1hi")
    form(1, 0, ROWS, *near)
    near = rows_for(3)
    arrived("q2lo")
    form(2, 0, ROWS, *near)
    acc[...] = jnp.dot(
        gt[:, : 3 * WIN], hc[0:3].reshape(3 * WIN, COLS), preferred_element_type=F32
    )
    own = ra2s[:, pl.ds(pl.multiple_of(z * 128, 128), 128)]
    for d in range(1, NZ):
        arrived(f"za{d}")
        own = own + ra2[d]
    fin[0, 0:QTR, :] = own.astype(BF16)
    own = rb2s[pl.ds(pl.multiple_of(h * TOK + c * QTR, QTR), QTR), :]
    for d in range(1, NY):
        arrived(f"yb{d}")
        own = own + rb2[d]
    fin[0, QTR:HALF, :] = own.astype(BF16)
    send("fin", fin.at[0], fin.at[1], fin.at[1], partner)
    across = rows_for(2)
    arrived("q3lo")
    arrived("q3hi")
    form(3, 0, ROWS, *across)
    head_ref[...] = (
        acc[...] + jnp.dot(gt[:, 3 * WIN :], hc[3], preferred_element_type=F32)
    ).astype(BF16)

    arrived("fin")
    for slot, row in ((0, k), (1, 1 - k)):
        value = fin[slot].astype(F32)
        value = jnp.where(k == 0, value[:, :64], value[:, 64:])
        hg_ref[0, pl.ds(pl.multiple_of(row * HALF, HALF), HALF), :] = value.astype(BF16)
    drain()


def body(*args):
    vmem = pl.BlockSpec(memory_space=pltpu.VMEM)
    hbm = pl.BlockSpec(memory_space=pltpu.HBM)
    dma = pltpu.SemaphoreType.DMA
    return pl.pallas_call(
        kernel,
        out_shape=(
            jax.ShapeDtypeStruct((1, TOK, D // (NH * NZ * 2)), BF16),
            jax.ShapeDtypeStruct((ROWS, COLS), BF16),
        ),
        in_specs=[hbm] * 8,
        out_specs=(vmem, vmem),
        scratch_shapes=[
            pltpu.VMEM((ROWS, D), BF16),
            pltpu.VMEM((WIN, D), BF16),
            pltpu.VMEM((NX, WIN, COLS), BF16),
            pltpu.VMEM((ROWS, WIN), F32),
            pltpu.VMEM((NX, ROWS, WIN), BF16),
            pltpu.VMEM((ROWS, NX * WIN), BF16),
            pltpu.VMEM((WIN, ROWS), BF16),
            pltpu.VMEM((WIN // 2, D), F32),
            pltpu.VMEM((WIN // 2, D), BF16),
            pltpu.VMEM((WIN // 2, D), BF16),
            pltpu.VMEM((NC, QTR, D), BF16),
            pltpu.VMEM((NZ, NH * TOK, 128), BF16),
            pltpu.VMEM((NY, QTR, D // NH), BF16),
            pltpu.VMEM((NZ, NH * TOK, 128), BF16),
            pltpu.VMEM((QTR, D // NH), F32),
            pltpu.VMEM((NH * TOK, 128), F32),
            pltpu.VMEM((NZ, QTR, 128), F32),
            pltpu.VMEM((NY, QTR, 128), F32),
            pltpu.VMEM((2, HALF, 128), BF16),
            pltpu.VMEM((2, 8, 128), F32),
            pltpu.VMEM((NY, 8, 128), F32),
            pltpu.VMEM((NZ, 8, 128), F32),
            pltpu.VMEM((NX, 8, 128), F32),
            pltpu.VMEM((ROWS, COLS), F32),
            pltpu.VMEM((1, WIN), jnp.int32),
            pltpu.VMEM((1, WIN), jnp.int32),
            pltpu.VMEM((1, WIN), jnp.int32),
            pltpu.VMEM((1, WIN), F32),
            pltpu.VMEM((1, WIN), F32),
            pltpu.VMEM((1, 8), F32),
            dma((8,)),
            dma((SEMS,)),
            dma((SEMS,)),
        ],
        compiler_params=pltpu.CompilerParams(
            collective_id=0, has_side_effects=True, vmem_limit_bytes=60 * 1024 * 1024
        ),
        cost_estimate=pl.CostEstimate(
            flops=6 * WIN * D * ROWS, bytes_accessed=2 * ROWS * (D + COLS), transcendentals=4 * ROWS * WIN
        ),
    )(*args)


def solution(mesh):
    placed = (P("dp", "ctx", None), P(("ctx", "vocab"), None)) + (P("dp", None),) * 6
    return jax.shard_map(
        body,
        mesh=mesh,
        in_specs=placed,
        out_specs=(P("dp", "ctx", "vocab"), P(("ctx", "vocab"), "dp")),
        check_vma=False,
    )
```

```python
import functools

import jax
import jax.numpy as jnp
from jax import lax
from jax.experimental import pallas as pl
from jax.experimental.pallas import tpu as pltpu
from jax.sharding import PartitionSpec as P

CLIP_LOW = 0.2
CLIP_HIGH = 0.28
DUAL_CLIP = 3.0
KL_COEF = 0.04
KL_CAP = 10.0
LOSS_SCALE = 64.0

MESH = pl.DeviceIdType.MESH
F32 = jnp.float32
BF16 = jnp.bfloat16

NX = 4
NC = 4
NH = 2
NY = NC * NH
NZ = 8
WIN = 256
TOK = WIN // NC
HALF = TOK // 2
QTR = HALF // 2
D = 2048
ROWS = 896
CH = 128
COLS = D // NX
PART = 512
NPART = D // PART
SPLIT = ROWS // 2


def token_weights(logp, mask, seq, old, ref, adv_ref):
    adv = jnp.zeros_like(logp)
    length = jnp.zeros_like(logp)
    for s in range(adv_ref.shape[1]):
        match = (seq == s).astype(F32)
        count = jnp.sum(match, axis=1, keepdims=True)
        adv = adv + match * adv_ref[0:1, s : s + 1]
        length = length + match * count
    ratio = jnp.exp(logp - old)
    low = jnp.where(ratio >= 1.0 - CLIP_LOW, jnp.where(ratio <= DUAL_CLIP, 1.0, 0.0), 0.0)
    active = jnp.where(adv >= 0.0, jnp.where(ratio <= 1.0 + CLIP_HIGH, 1.0, 0.0), low)
    policy = jnp.where(active > 0.0, -adv * ratio, 0.0)
    gap = ref - logp
    exp_gap = jnp.exp(gap)
    penalty = jnp.where(exp_gap - gap - 1.0 < KL_CAP, 1.0 - exp_gap, 0.0)
    return LOSS_SCALE * mask.astype(F32) * (policy + KL_COEF * penalty) / length


def merge(ref, n):
    top = ref[0, 0:2, :]
    for i in range(1, n):
        top = jnp.maximum(top, ref[i, 0:2, :])
    total = jnp.zeros_like(top)
    label = jnp.zeros_like(top)
    for i in range(n):
        total = total + ref[i, 2:4, :] * jnp.exp(ref[i, 0:2, :] - top)
        label = label + ref[i, 4:6, :]
    return top, total, label


def turn(rows, out):
    rows = list(rows) + [jnp.zeros_like(rows[0])] * (8 - len(rows))
    out[...] = jnp.concatenate(rows, axis=0).T


def put(ref, slot, top, total, label):
    ref[slot] = jnp.concatenate([top, total, label, jnp.zeros_like(top)], axis=0)


def fold(row):
    return jnp.concatenate([row[:, :128], row[:, 128:]], axis=0)


def unfold(tile):
    return jnp.concatenate([tile[0:1, :], tile[1:2, :]], axis=1)


SEMS = 140


def kernel(
    hid_hbm,
    w_hbm,
    lab_hbm,
    mask_hbm,
    seq_hbm,
    old_hbm,
    refp_hbm,
    adv_hbm,
    hg_ref,
    head_ref,
    w,
    win,
    hc,
    logit,
    q,
    gt,
    g,
    keep,
    e1s,
    e1r,
    keepl,
    els,
    elr,
    rsa,
    rsb,
    rsl,
    ra1,
    rb1,
    rl1,
    ra2s,
    rb2s,
    rl2s,
    ra2,
    rb2,
    rl2,
    fin,
    st0,
    sty,
    stz,
    styz,
    stzy,
    scale,
    col0,
    col1a,
    col1b,
    col2a,
    col2b,
    coll,
    acc,
    lab_ref,
    mask_ref,
    seq_ref,
    old_ref,
    refp_ref,
    adv_ref,
    loc_sem,
    send_sems,
    recv_sems,
):
    x = lax.axis_index("dp")
    c = lax.axis_index("ctx")
    v = lax.axis_index("vocab")
    h = v // (NZ * 2)
    z = (v // 2) % NZ
    k = v % 2
    y = h * NC + c

    def at_y(to):
        return (x, to % NC, (to // NC) * (NZ * 2) + z * 2 + k)

    def at_z(to):
        return (x, c, h * (NZ * 2) + to * 2 + k)

    def at_x(to):
        return (to, c, v)

    partner = (x, c, h * (NZ * 2) + z * 2 + (1 - k))

    sent = []
    coming = {}

    def send(name, src, dst, landing, to):
        at = len(sent)
        copy = pltpu.make_async_remote_copy(
            src_ref=src,
            dst_ref=dst,
            send_sem=send_sems.at[at],
            recv_sem=recv_sems.at[at],
            device_id=to,
            device_id_type=MESH,
        )
        copy.start()
        sent.append(copy)
        coming[name] = pltpu.make_async_remote_copy(
            src_ref=landing,
            dst_ref=landing,
            send_sem=send_sems.at[at],
            recv_sem=recv_sems.at[at],
            device_id=to,
            device_id_type=MESH,
        )

    def arrived(name):
        coming.pop(name).wait_recv()

    def drain():
        for name in list(coming):
            arrived(name)
        for copy in sent:
            copy.wait_send()

    block = pl.ds(pl.multiple_of(c * TOK, TOK), TOK)
    load_hid = pltpu.make_async_copy(hid_hbm.at[0], win.at[block, :], loc_sem.at[0])
    load_hid.start()
    load_w = pltpu.make_async_copy(w_hbm, w, loc_sem.at[1])
    load_w.start()
    loads = []
    for i, (src, dst) in enumerate(
        (
            (lab_hbm, lab_ref),
            (mask_hbm, mask_ref),
            (seq_hbm, seq_ref),
            (old_hbm, old_ref),
            (refp_hbm, refp_ref),
            (adv_hbm, adv_ref),
        )
    ):
        loads.append(pltpu.make_async_copy(src, dst, loc_sem.at[2 + i]))
        loads[-1].start()

    barrier = pltpu.get_barrier_semaphore()
    peers = [partner]
    peers += [at_y((y + d) % NY) for d in range(1, NY)]
    peers += [at_z((z + d) % NZ) for d in range(1, NZ)]
    peers += [at_x((x + d) % NX) for d in range(1, NX)]
    for peer in peers:
        pl.semaphore_signal(barrier, inc=1, device_id=peer, device_id_type=MESH)
    pl.semaphore_wait(barrier, len(peers))

    def half_rows(number, half):
        return pl.ds(pl.multiple_of(number * TOK + half * HALF, HALF), HALF)

    def rows_of(i):
        return pl.ds(pl.multiple_of(i * CH, CH), CH)

    place = {0: 0, 1: 1, 3: 2, 2: 3}
    right, left = (x + 1) % NX, (x + NX - 1) % NX

    far = (y + NY + 2 - 4 * k) % NY
    from_block = ((c + NC - 1) % NC, (c + 1) % NC, (c + 2) % NC)
    mine = hid_hbm.at[0, pl.ds(pl.multiple_of(k * HALF, HALF), HALF), :]
    for i, to in enumerate(((y + 1) % NY, (y + NY - 1) % NY, far)):
        send(
            f"a{i}", mine, win.at[half_rows(c, k), :], win.at[half_rows(from_block[i], k), :], at_y(to)
        )

    def spread_columns(i, number, src):
        for d in (1, 3, 2):
            to = (x + d) % NX
            part = src.at[:, pl.ds(pl.multiple_of(to * COLS, COLS), COLS)]
            dst = hc.at[place[d], half_rows(number, k), :]
            send(f"h{i}{d}", part, dst, dst, at_x(to))

    spread_columns(3, c, mine)

    load_w.wait()
    for load in loads:
        load.wait()
    base = (c * (NH * NZ * 2) + v) * ROWS
    local_label = lab_ref[...] - base

    def hit(i):
        rows = lax.broadcasted_iota(jnp.int32, (CH, WIN), 0) + i * CH
        return rows == local_label

    def put_turned(i, value):
        turned = value.T.astype(BF16)
        for j in range(NC):
            for half in range(2):
                row = j * HALF + (WIN // 2) * (1 - k if half == 0 else k)
                start = j * TOK + half * HALF
                g[pl.ds(pl.multiple_of(row, HALF), HALF), rows_of(i)] = turned[start : start + HALF]

    def label_step(i, carry):
        put_turned(i, hit(i).astype(F32))
        return carry

    lax.fori_loop(0, ROWS // CH, label_step, 0)
    for n in range(NPART):
        cols = pl.ds(n * PART, PART)
        value = jnp.dot(g[...], w[:, n * PART : (n + 1) * PART], preferred_element_type=F32)
        els[:, cols] = value[: WIN // 2].astype(BF16)
        keepl[:, cols] = value[WIN // 2 :].astype(BF16)
    send("l", els, elr, elr, partner)
    arrived("l")
    for j in range(NC):
        rows = slice(j * HALF, (j + 1) * HALF)
        both = (keepl[rows, :].astype(F32) + elr[rows, :].astype(F32)).astype(BF16)
        for m in range(D // 128):
            hh, zz = m // NZ, m % NZ
            rsl[zz, hh * (NC * HALF) + j * HALF : hh * (NC * HALF) + (j + 1) * HALF, :] = both[
                :, m * 128 : (m + 1) * 128
            ]
    for d in range(1, NZ):
        to = (z + d) % NZ
        send(f"zl{d}", rsl.at[to], rl1.at[d], rl1.at[d], at_z(to))

    for i in range(3):
        arrived(f"a{i}")
        piece = win.at[half_rows(from_block[i], k), :]
        send(f"f{i}", piece, piece, win.at[half_rows(from_block[i], 1 - k), :], partner)
        spread_columns(i, from_block[i], piece)
    load_hid.wait()
    for i in range(3):
        arrived(f"f{i}")
    logit[...] = lax.dot_general(
        w[...], win[...], (((1,), (1,)), ((), ())), preferred_element_type=F32
    )

    def stat_step(i, carry):
        top, label = carry
        part = logit[rows_of(i), :]
        here = hit(i)
        top = jnp.maximum(top, jnp.max(jnp.where(here, -jnp.inf, part), axis=0, keepdims=True))
        label = label + jnp.sum(jnp.where(here, part, 0.0), axis=0, keepdims=True)
        return top, label

    top, label = lax.fori_loop(
        0, ROWS // CH, stat_step, (jnp.full((1, WIN), -jnp.inf, F32), jnp.zeros((1, WIN), F32))
    )

    def exp_step(i, total):
        here = hit(i)
        part = jnp.where(here, 0.0, jnp.exp(logit[rows_of(i), :] - top))
        q[0, rows_of(i), :] = jnp.where(here, -1.0, part).astype(BF16)
        put_turned(i, part)
        return total + jnp.sum(part, axis=0, keepdims=True)

    total = lax.fori_loop(0, ROWS // CH, exp_step, jnp.zeros((1, WIN), F32))
    put(st0, k, fold(top), fold(total), fold(label))
    send("c", st0.at[k], st0.at[k], st0.at[1 - k], partner)

    lo, hi = pl.ds(0, SPLIT), pl.ds(SPLIT, SPLIT)
    send("q1lo", q.at[0, lo, :], q.at[1, lo, :], q.at[1, lo, :], at_x(right))
    send("q2hi", q.at[0, hi, :], q.at[2, hi, :], q.at[2, hi, :], at_x(left))
    for n in range(NPART):
        cols = pl.ds(n * PART, PART)
        value = jnp.dot(g[...], w[:, n * PART : (n + 1) * PART], preferred_element_type=F32)
        e1s[:, cols] = value[: WIN // 2].astype(BF16)
        keep[:, cols] = value[WIN // 2 :]
        send(f"e{n}", e1s.at[:, cols], e1r.at[:, cols], e1r.at[:, cols], partner)

    arrived("c")
    pair = merge(st0, 2)
    put(sty, y, *pair)
    put(stz, z, *pair)
    for d in range(1, NY):
        send(f"cy{d}", sty.at[y], sty.at[y], sty.at[(y + NY - d) % NY], at_y((y + d) % NY))
    for d in range(1, NZ):
        send(f"cz{d}", stz.at[z], stz.at[z], stz.at[(z + NZ - d) % NZ], at_z((z + d) % NZ))

    def relative(ref, slot, norm):
        return unfold(jnp.exp(ref[slot, 0:2, :] - norm))

    turn([relative(st0, k, pair[0]), relative(st0, 1 - k, pair[0])], col0)
    for n in range(NPART):
        cols = pl.ds(n * PART, PART)
        arrived(f"e{n}")
        for j in range(NC):
            rows = slice(j * HALF, (j + 1) * HALF)
            factors = col0[half_rows(j, k), :]
            both = keep[rows, n * PART : (n + 1) * PART] * factors[:, 0:1]
            both = both + e1r[rows, n * PART : (n + 1) * PART].astype(F32) * factors[:, 1:2]
            both = both.astype(BF16)
            rsa[j, :, cols] = both[:QTR]
            for m in range(PART // 128):
                block = n * (PART // 128) + m
                hh, zz = block // NZ, block % NZ
                rsb[zz, hh * TOK + j * QTR : hh * TOK + (j + 1) * QTR, :] = both[
                    QTR:, m * 128 : (m + 1) * 128
                ]

    for d in range(1, NY):
        to = (y + d) % NY
        src = rsa.at[to % NC, :, pl.ds(pl.multiple_of((to // NC) * (D // NH), D // NH), D // NH)]
        send(f"ya{d}", src, ra1.at[d], ra1.at[d], at_y(to))
        to = (z + d) % NZ
        send(f"zb{d}", rsb.at[to], rb1.at[d], rb1.at[d], at_z(to))
    send("q1hi", q.at[0, hi, :], q.at[1, hi, :], q.at[1, hi, :], at_x(right))
    send("q2lo", q.at[0, lo, :], q.at[2, lo, :], q.at[2, lo, :], at_x(left))
    own = rsl[z].astype(F32)
    for d in range(1, NZ):
        arrived(f"zl{d}")
        own = own + rl1[d].astype(F32)
    rl2s[...] = own.astype(BF16)
    for d in range(1, NY):
        to = (y + d) % NY
        src = rl2s.at[pl.ds(pl.multiple_of((to // NC) * (NC * HALF) + (to % NC) * HALF, HALF), HALF), :]
        send(f"yl{d}", src, rl2.at[d], rl2.at[d], at_y(to))

    for i, number in ((3, c), (0, from_block[0]), (1, from_block[1]), (2, from_block[2])):
        for d in (1, 3, 2):
            arrived(f"h{i}{d}")
            piece = hc.at[place[d], half_rows(number, k), :]
            send(f"g{i}{d}", piece, piece, hc.at[place[d], half_rows(number, 1 - k), :], partner)
    hc[0] = win[:, pl.ds(pl.multiple_of(x * COLS, COLS), COLS)]

    for d in range(1, NY):
        arrived(f"cy{d}")
    ring_y = merge(sty, NY)
    put(styz, z, *ring_y)
    for d in range(1, NZ):
        send(f"cyz{d}", styz.at[z], styz.at[z], styz.at[(z + NZ - d) % NZ], at_z((z + d) % NZ))
    for d in range(1, NZ):
        arrived(f"cz{d}")
    ring_z = merge(stz, NZ)
    put(stzy, y, *ring_z)
    for d in range(1, NY):
        send(f"czy{d}", stzy.at[y], stzy.at[y], stzy.at[(y + NY - d) % NY], at_y((y + d) % NY))
    turn([relative(sty, (y + NY - d) % NY, ring_y[0]) for d in range(NY)], col1a)
    turn([relative(stz, (z + NZ - d) % NZ, ring_z[0]) for d in range(NZ)], col1b)

    arrived("q1lo")
    send("q3lo", q.at[1, lo, :], q.at[3, lo, :], q.at[3, lo, :], at_x(right))
    arrived("q2hi")
    send("q3hi", q.at[2, hi, :], q.at[3, hi, :], q.at[3, hi, :], at_x(left))
    rows_a = pl.ds(pl.multiple_of(c * TOK + k * HALF, QTR), QTR)
    rows_b = pl.ds(pl.multiple_of(c * TOK + k * HALF + QTR, QTR), QTR)
    factors = col1a[rows_a, :]
    own = rsa[c, :, pl.ds(pl.multiple_of(h * (D // NH), D // NH), D // NH)].astype(F32) * factors[:, 0:1]
    for d in range(1, NY):
        arrived(f"ya{d}")
        own = own + ra1[d].astype(F32) * factors[:, d : d + 1]
    ra2s[...] = own
    for d in range(1, NZ):
        to = (z + d) % NZ
        src = ra2s.at[:, pl.ds(pl.multiple_of(to * 128, 128), 128)]
        send(f"za{d}", src, ra2.at[d], ra2.at[d], at_z(to))
    factors = [
        col1b[pl.ds(pl.multiple_of(j * TOK + k * HALF + QTR, QTR), QTR), :] for j in range(NC)
    ]
    factors = jnp.concatenate(factors + factors, axis=0)
    own = rsb[z].astype(F32) * factors[:, 0:1]
    for d in range(1, NZ):
        arrived(f"zb{d}")
        own = own + rb1[d].astype(F32) * factors[:, d : d + 1]
    rb2s[...] = own
    for d in range(1, NY):
        to = (y + d) % NY
        src = rb2s.at[pl.ds(pl.multiple_of((to // NC) * TOK + (to % NC) * QTR, QTR), QTR), :]
        send(f"yb{d}", src, rb2.at[d], rb2.at[d], at_y(to))
    for d in range(1, NZ):
        arrived(f"cyz{d}")
    all_top, all_rest, all_label = merge(styz, NZ)
    peak = jnp.maximum(all_top, all_label)
    rest = all_rest * jnp.exp(all_top - peak)
    whole = rest + jnp.exp(all_label - peak)
    log_total = peak + jnp.log(whole)
    row_total = unfold(log_total)
    coeff = token_weights(
        unfold(all_label - log_total), mask_ref[...], seq_ref[...], old_ref[...], refp_ref[...], adv_ref
    )
    factor = coeff * jnp.exp(top - row_total)
    label_grad = coeff * unfold(rest / whole)
    put(scale, 0, fold(factor), fold(label_grad), fold(label_grad))
    for d in (1, 3, 2):
        send(f"x{d}", scale.at[0], scale.at[d], scale.at[d], at_x((x + d) % NX))

    def form(slot, factor_row, label_row):
        def step(i, carry):
            part = q[slot, rows_of(i), :].astype(F32)
            grad = jnp.where(part < 0.0, label_row, -part * factor_row)
            gt[rows_of(i), slot * WIN : (slot + 1) * WIN] = grad.astype(BF16)
            return carry

        lax.fori_loop(0, ROWS // CH, step, 0)

    def rows_for(d):
        arrived(f"x{d}")
        return unfold(scale[d, 0:2, :]), unfold(scale[d, 2:4, :])

    form(0, factor, label_grad)
    for d in range(1, NY):
        arrived(f"czy{d}")
    turn([-coeff * relative(styz, (z + NZ - d) % NZ, log_total) for d in range(NZ)], col2a)
    turn([-coeff * relative(stzy, (y + NY - d) % NY, log_total) for d in range(NY)], col2b)
    turn([label_grad], coll)
    own = rl2s[pl.ds(pl.multiple_of(h * (NC * HALF) + c * HALF, HALF), HALF), :].astype(F32)
    for d in range(1, NY):
        arrived(f"yl{d}")
        own = own + rl2[d].astype(F32)
    own_label = own * coll[half_rows(c, k), :][:, 0:1]

    for i in range(4):
        for d in (1, 3, 2):
            arrived(f"g{i}{d}")
    near = rows_for(1)
    arrived("q1hi")
    form(1, *near)
    near = rows_for(3)
    arrived("q2lo")
    form(2, *near)
    acc[...] = jnp.dot(
        gt[:, : 3 * WIN], hc[0:3].reshape(3 * WIN, COLS), preferred_element_type=F32
    )

    factors = col2a[rows_a, :]
    own = own_label[:QTR]
    own = own + ra2s[:, pl.ds(pl.multiple_of(z * 128, 128), 128)] * factors[:, 0:1]
    for d in range(1, NZ):
        arrived(f"za{d}")
        own = own + ra2[d] * factors[:, d : d + 1]
    fin[0, 0:QTR, :] = own.astype(BF16)
    factors = col2b[rows_b, :]
    own = own_label[QTR:]
    own = own + rb2s[pl.ds(pl.multiple_of(h * TOK + c * QTR, QTR), QTR), :] * factors[:, 0:1]
    for d in range(1, NY):
        arrived(f"yb{d}")
        own = own + rb2[d] * factors[:, d : d + 1]
    fin[0, QTR:HALF, :] = own.astype(BF16)
    send("fin", fin.at[0], fin.at[1], fin.at[1], partner)
    across = rows_for(2)
    arrived("q3lo")
    arrived("q3hi")
    form(3, *across)
    head_ref[...] = (
        acc[...] + jnp.dot(gt[:, 3 * WIN :], hc[3], preferred_element_type=F32)
    ).astype(BF16)

    arrived("fin")
    for slot, row in ((0, k), (1, 1 - k)):
        value = fin[slot].astype(F32)
        value = jnp.where(k == 0, value[:, :64], value[:, 64:])
        hg_ref[0, pl.ds(pl.multiple_of(row * HALF, HALF), HALF), :] = value.astype(BF16)
    drain()


def body(*args):
    vmem = pl.BlockSpec(memory_space=pltpu.VMEM)
    hbm = pl.BlockSpec(memory_space=pltpu.HBM)
    dma = pltpu.SemaphoreType.DMA
    args = [pltpu.with_memory_space_constraint(a, pltpu.HBM) for a in args]
    return pl.pallas_call(
        kernel,
        out_shape=(
            pltpu.VMEM((1, TOK, D // (NH * NZ * 2)), BF16),
            pltpu.VMEM((ROWS, COLS), BF16),
        ),
        in_specs=[hbm] * 8,
        out_specs=(vmem, vmem),
        scratch_shapes=[
            pltpu.VMEM((ROWS, D), BF16),
            pltpu.VMEM((WIN, D), BF16),
            pltpu.VMEM((NX, WIN, COLS), BF16),
            pltpu.VMEM((ROWS, WIN), F32),
            pltpu.VMEM((NX, ROWS, WIN), BF16),
            pltpu.VMEM((ROWS, NX * WIN), BF16),
            pltpu.VMEM((WIN, ROWS), BF16),
            pltpu.VMEM((WIN // 2, D), F32),
            pltpu.VMEM((WIN // 2, D), BF16),
            pltpu.VMEM((WIN // 2, D), BF16),
            pltpu.VMEM((WIN // 2, D), BF16),
            pltpu.VMEM((WIN // 2, D), BF16),
            pltpu.VMEM((WIN // 2, D), BF16),
            pltpu.VMEM((NC, QTR, D), BF16),
            pltpu.VMEM((NZ, NH * TOK, 128), BF16),
            pltpu.VMEM((NZ, NH * NC * HALF, 128), BF16),
            pltpu.VMEM((NY, QTR, D // NH), BF16),
            pltpu.VMEM((NZ, NH * TOK, 128), BF16),
            pltpu.VMEM((NZ, NH * NC * HALF, 128), BF16),
            pltpu.VMEM((QTR, D // NH), F32),
            pltpu.VMEM((NH * TOK, 128), F32),
            pltpu.VMEM((NH * NC * HALF, 128), BF16),
            pltpu.VMEM((NZ, QTR, 128), F32),
            pltpu.VMEM((NY, QTR, 128), F32),
            pltpu.VMEM((NY, HALF, 128), BF16),
            pltpu.VMEM((2, HALF, 128), BF16),
            pltpu.VMEM((2, 8, 128), F32),
            pltpu.VMEM((NY, 8, 128), F32),
            pltpu.VMEM((NZ, 8, 128), F32),
            pltpu.VMEM((NZ, 8, 128), F32),
            pltpu.VMEM((NY, 8, 128), F32),
            pltpu.VMEM((NX, 8, 128), F32),
            pltpu.VMEM((WIN, 8), F32),
            pltpu.VMEM((WIN, 8), F32),
            pltpu.VMEM((WIN, 8), F32),
            pltpu.VMEM((WIN, 8), F32),
            pltpu.VMEM((WIN, 8), F32),
            pltpu.VMEM((WIN, 8), F32),
            pltpu.VMEM((ROWS, COLS), F32),
            pltpu.VMEM((1, WIN), jnp.int32),
            pltpu.VMEM((1, WIN), jnp.int32),
            pltpu.VMEM((1, WIN), jnp.int32),
            pltpu.VMEM((1, WIN), F32),
            pltpu.VMEM((1, WIN), F32),
            pltpu.VMEM((1, 8), F32),
            dma((8,)),
            dma((SEMS,)),
            dma((SEMS,)),
        ],
        compiler_params=pltpu.CompilerParams(
            collective_id=0, has_side_effects=True, vmem_limit_bytes=48 * 1024 * 1024
        ),
        cost_estimate=pl.CostEstimate(
            flops=8 * WIN * D * ROWS, bytes_accessed=2 * ROWS * (D + COLS), transcendentals=4 * ROWS * WIN
        ),
    )(*args)


def solution(mesh):
    placed = (P("dp", "ctx", None), P(("ctx", "vocab"), None)) + (P("dp", None),) * 6
    return jax.shard_map(
        body,
        mesh=mesh,
        in_specs=placed,
        out_specs=(P("dp", "ctx", "vocab"), P(("ctx", "vocab"), "dp")),
        check_vma=False,
    )
```

```python
import functools

import jax
import jax.numpy as jnp
from jax import lax
from jax.experimental import pallas as pl
from jax.experimental.pallas import tpu as pltpu
from jax.sharding import PartitionSpec as P

CLIP_LOW = 0.2
CLIP_HIGH = 0.28
DUAL_CLIP = 3.0
KL_COEF = 0.04
KL_CAP = 10.0
LOSS_SCALE = 64.0

MESH = pl.DeviceIdType.MESH
F32 = jnp.float32
BF16 = jnp.bfloat16

NX = 4
NC = 4
NH = 2
NY = NC * NH
NZ = 8
WIN = 256
TOK = WIN // NC
HALF = TOK // 2
QTR = HALF // 2
D = 2048
ROWS = 896
CH = 128
COLS = D // NX
PART = 512
NPART = D // PART
SPLIT = ROWS // 2


def token_weights(logp, mask, seq, old, ref, adv_ref):
    adv = jnp.zeros_like(logp)
    length = jnp.zeros_like(logp)
    for s in range(adv_ref.shape[1]):
        match = (seq == s).astype(F32)
        count = jnp.sum(match, axis=1, keepdims=True)
        adv = adv + match * adv_ref[0:1, s : s + 1]
        length = length + match * count
    ratio = jnp.exp(logp - old)
    low = jnp.where(ratio >= 1.0 - CLIP_LOW, jnp.where(ratio <= DUAL_CLIP, 1.0, 0.0), 0.0)
    active = jnp.where(adv >= 0.0, jnp.where(ratio <= 1.0 + CLIP_HIGH, 1.0, 0.0), low)
    policy = jnp.where(active > 0.0, -adv * ratio, 0.0)
    gap = ref - logp
    exp_gap = jnp.exp(gap)
    penalty = jnp.where(exp_gap - gap - 1.0 < KL_CAP, 1.0 - exp_gap, 0.0)
    return LOSS_SCALE * mask.astype(F32) * (policy + KL_COEF * penalty) / length


def merge(ref, n):
    top = ref[0, 0:2, :]
    for i in range(1, n):
        top = jnp.maximum(top, ref[i, 0:2, :])
    total = jnp.zeros_like(top)
    label = jnp.zeros_like(top)
    for i in range(n):
        total = total + ref[i, 2:4, :] * jnp.exp(ref[i, 0:2, :] - top)
        label = label + ref[i, 4:6, :]
    return top, total, label


def turn(rows, out):
    rows = list(rows) + [jnp.zeros_like(rows[0])] * (8 - len(rows))
    out[...] = jnp.concatenate(rows, axis=0).T


def put(ref, slot, top, total, label):
    ref[slot] = jnp.concatenate([top, total, label, jnp.zeros_like(top)], axis=0)


def fold(row):
    return jnp.concatenate([row[:, :128], row[:, 128:]], axis=0)


def unfold(tile):
    return jnp.concatenate([tile[0:1, :], tile[1:2, :]], axis=1)


SEMS = 140
BLOCK = 448
FAR = (4, 3, 5, 2, 6, 1, 7)


def kernel(
    hid_hbm,
    w_hbm,
    lab_hbm,
    mask_hbm,
    seq_hbm,
    old_hbm,
    refp_hbm,
    adv_hbm,
    hg_ref,
    head_ref,
    w,
    win,
    hc,
    logit,
    q,
    gt,
    g,
    keep,
    e1s,
    e1r,
    keepl,
    els,
    elr,
    rsa,
    rsb,
    rsl,
    ra1,
    rb1,
    rl1,
    ra2s,
    rb2s,
    rl2s,
    ra2,
    rb2,
    rl2,
    fin,
    st0,
    sty,
    stz,
    styz,
    stzy,
    scale,
    col0,
    col1a,
    col1b,
    col2a,
    col2b,
    coll,
    lab_ref,
    mask_ref,
    seq_ref,
    old_ref,
    refp_ref,
    adv_ref,
    loc_sem,
    send_sems,
    recv_sems,
):
    x = lax.axis_index("dp")
    c = lax.axis_index("ctx")
    v = lax.axis_index("vocab")
    h = v // (NZ * 2)
    z = (v // 2) % NZ
    k = v % 2
    y = h * NC + c

    def at_y(to):
        return (x, to % NC, (to // NC) * (NZ * 2) + z * 2 + k)

    def at_z(to):
        return (x, c, h * (NZ * 2) + to * 2 + k)

    def at_x(to):
        return (to, c, v)

    partner = (x, c, h * (NZ * 2) + z * 2 + (1 - k))

    sent = []
    coming = {}
    names = []
    settled = set()

    def send(name, src, dst, landing, to):
        at = len(sent)
        copy = pltpu.make_async_remote_copy(
            src_ref=src,
            dst_ref=dst,
            send_sem=send_sems.at[at],
            recv_sem=recv_sems.at[at],
            device_id=to,
            device_id_type=MESH,
        )
        copy.start()
        sent.append(copy)
        names.append(name)
        coming[name] = pltpu.make_async_remote_copy(
            src_ref=landing,
            dst_ref=landing,
            send_sem=send_sems.at[at],
            recv_sem=recv_sems.at[at],
            device_id=to,
            device_id_type=MESH,
        )

    def arrived(name):
        coming.pop(name).wait_recv()

    def drain():
        for name in list(coming):
            arrived(name)
        settle(())

    def settle(later):
        for at, copy in enumerate(sent):
            if at not in settled and not (later and names[at].startswith(later)):
                copy.wait_send()
                settled.add(at)

    block = pl.ds(pl.multiple_of(c * TOK, TOK), TOK)
    load_hid = pltpu.make_async_copy(hid_hbm.at[0], win.at[block, :], loc_sem.at[0])
    load_hid.start()
    load_w = pltpu.make_async_copy(w_hbm, w, loc_sem.at[1])
    load_w.start()
    loads = []
    for i, (src, dst) in enumerate(
        (
            (lab_hbm, lab_ref),
            (mask_hbm, mask_ref),
            (seq_hbm, seq_ref),
            (old_hbm, old_ref),
            (refp_hbm, refp_ref),
            (adv_hbm, adv_ref),
        )
    ):
        loads.append(pltpu.make_async_copy(src, dst, loc_sem.at[2 + i]))
        loads[-1].start()

    barrier = pltpu.get_barrier_semaphore()
    peers = [partner]
    peers += [at_y((y + d) % NY) for d in range(1, NY)]
    peers += [at_z((z + d) % NZ) for d in range(1, NZ)]
    peers += [at_x((x + d) % NX) for d in range(1, NX)]
    for peer in peers:
        pl.semaphore_signal(barrier, inc=1, device_id=peer, device_id_type=MESH)
    pl.semaphore_wait(barrier, len(peers))

    def half_rows(number, half):
        return pl.ds(pl.multiple_of(number * TOK + half * HALF, HALF), HALF)

    def rows_of(i):
        return pl.ds(pl.multiple_of(i * CH, CH), CH)

    place = {0: 0, 1: 1, 3: 2, 2: 3}
    right, left = (x + 1) % NX, (x + NX - 1) % NX

    far = (y + NY + 2 - 4 * k) % NY
    from_block = ((c + NC - 1) % NC, (c + 1) % NC, (c + 2) % NC)
    mine = hid_hbm.at[0, pl.ds(pl.multiple_of(k * HALF, HALF), HALF), :]
    for i, to in ((2, far), (0, (y + 1) % NY), (1, (y + NY - 1) % NY)):
        send(
            f"a{i}", mine, win.at[half_rows(c, k), :], win.at[half_rows(from_block[i], k), :], at_y(to)
        )

    def spread_columns(i, number, src):
        for d in (1, 3, 2):
            to = (x + d) % NX
            part = src.at[:, pl.ds(pl.multiple_of(to * COLS, COLS), COLS)]
            dst = hc.at[place[d], half_rows(number, k), :]
            send(f"h{i}{d}", part, dst, dst, at_x(to))

    spread_columns(3, c, mine)

    load_w.wait()
    for load in loads:
        load.wait()
    base = (c * (NH * NZ * 2) + v) * ROWS
    local_label = lab_ref[...] - base

    def hit(i):
        rows = lax.broadcasted_iota(jnp.int32, (CH, WIN), 0) + i * CH
        return rows == local_label

    def put_turned(i, value):
        turned = value.T.astype(BF16)
        for j in range(NC):
            for half in range(2):
                row = j * HALF + (WIN // 2) * (1 - k if half == 0 else k)
                start = j * TOK + half * HALF
                g[pl.ds(pl.multiple_of(row, HALF), HALF), rows_of(i)] = turned[start : start + HALF]

    def label_step(i, carry):
        put_turned(i, hit(i).astype(F32))
        return carry

    lax.fori_loop(0, ROWS // CH, label_step, 0)

    def part_cols(n):
        return pl.ds(pl.multiple_of(n * PART, PART), PART)

    def label_dot(n, carry):
        cols = part_cols(n)
        value = jnp.dot(g[...], w[:, cols], preferred_element_type=F32)
        els[:, cols] = value[: WIN // 2].astype(BF16)
        keepl[:, cols] = value[WIN // 2 :].astype(BF16)
        return carry

    lax.fori_loop(0, NPART, label_dot, 0)
    send("l", els, elr, elr, partner)
    arrived("l")

    def label_merge(j, carry):
        rows = pl.ds(pl.multiple_of(j * HALF, HALF), HALF)
        both = (keepl[rows, :].astype(F32) + elr[rows, :].astype(F32)).astype(BF16)
        for m in range(D // 128):
            hh, zz = m // NZ, m % NZ
            rows = pl.ds(pl.multiple_of(hh * (NC * HALF) + j * HALF, HALF), HALF)
            rsl[zz, rows, :] = both[:, m * 128 : (m + 1) * 128]
        return carry

    lax.fori_loop(0, NC, label_merge, 0)
    for d in FAR:
        to = (z + d) % NZ
        send(f"zl{d}", rsl.at[to], rl1.at[d], rl1.at[d], at_z(to))

    for i in range(3):
        arrived(f"a{i}")
        piece = win.at[half_rows(from_block[i], k), :]
        send(f"f{i}", piece, piece, win.at[half_rows(from_block[i], 1 - k), :], partner)
        spread_columns(i, from_block[i], piece)
    load_hid.wait()
    for i in range(3):
        arrived(f"f{i}")
    def block_rows(i):
        return pl.ds(pl.multiple_of(i * BLOCK, BLOCK), BLOCK)

    def logit_step(i, carry):
        logit[block_rows(i), :] = lax.dot_general(
            w[block_rows(i), :], win[...], (((1,), (1,)), ((), ())), preferred_element_type=F32
        )
        return carry

    lax.fori_loop(0, ROWS // BLOCK, logit_step, 0)

    def stat_step(i, carry):
        top, label = carry
        part = logit[rows_of(i), :]
        here = hit(i)
        top = jnp.maximum(top, jnp.max(jnp.where(here, -jnp.inf, part), axis=0, keepdims=True))
        label = label + jnp.sum(jnp.where(here, part, 0.0), axis=0, keepdims=True)
        return top, label

    top, label = lax.fori_loop(
        0, ROWS // CH, stat_step, (jnp.full((1, WIN), -jnp.inf, F32), jnp.zeros((1, WIN), F32))
    )

    def exp_step(i, total):
        here = hit(i)
        part = jnp.where(here, 0.0, jnp.exp(logit[rows_of(i), :] - top))
        q[0, rows_of(i), :] = jnp.where(here, -1.0, part).astype(BF16)
        put_turned(i, part)
        return total + jnp.sum(part, axis=0, keepdims=True)

    total = lax.fori_loop(0, ROWS // CH, exp_step, jnp.zeros((1, WIN), F32))
    put(st0, k, fold(top), fold(total), fold(label))
    send("c", st0.at[k], st0.at[k], st0.at[1 - k], partner)

    lo, hi = pl.ds(0, SPLIT), pl.ds(SPLIT, SPLIT)
    send("q1lo", q.at[0, lo, :], q.at[1, lo, :], q.at[1, lo, :], at_x(right))
    send("q2hi", q.at[0, hi, :], q.at[2, hi, :], q.at[2, hi, :], at_x(left))
    first = len(sent)

    def swap(n):
        return pltpu.make_async_remote_copy(
            src_ref=e1s.at[:, part_cols(n)],
            dst_ref=e1r.at[:, part_cols(n)],
            send_sem=send_sems.at[first + n],
            recv_sem=recv_sems.at[first + n],
            device_id=partner,
            device_id_type=MESH,
        )

    def weight_sums(n, carry):
        cols = part_cols(n)
        value = jnp.dot(g[...], w[:, cols], preferred_element_type=F32)
        e1s[:, cols] = value[: WIN // 2].astype(BF16)
        keep[:, cols] = value[WIN // 2 :]
        swap(n).start()
        return carry

    lax.fori_loop(0, NPART, weight_sums, 0)
    sent.extend(swap(n) for n in range(NPART))
    names.extend("e" for n in range(NPART))

    arrived("c")
    pair = merge(st0, 2)
    put(sty, y, *pair)
    put(stz, z, *pair)
    for d in FAR:
        send(f"cy{d}", sty.at[y], sty.at[y], sty.at[(y + NY - d) % NY], at_y((y + d) % NY))
    for d in FAR:
        send(f"cz{d}", stz.at[z], stz.at[z], stz.at[(z + NZ - d) % NZ], at_z((z + d) % NZ))

    def relative(ref, slot, norm):
        return unfold(jnp.exp(ref[slot, 0:2, :] - norm))

    turn([relative(st0, k, pair[0]), relative(st0, 1 - k, pair[0])], col0)

    def pair_merge(n, carry):
        cols = part_cols(n)
        swap(n).wait_recv()
        for j in range(NC):
            rows = slice(j * HALF, (j + 1) * HALF)
            factors = col0[half_rows(j, k), :]
            both = keep[rows, cols] * factors[:, 0:1] + e1r[rows, cols].astype(F32) * factors[:, 1:2]
            both = both.astype(BF16)
            rsa[j, :, cols] = both[:QTR]
            for m in range(PART // 128):
                hh, zz = n // (NPART // NH), n % (NPART // NH) * (PART // 128) + m
                rows_b = pl.ds(pl.multiple_of(hh * TOK + j * QTR, QTR), QTR)
                rsb[zz, rows_b, :] = both[QTR:, m * 128 : (m + 1) * 128]
        return carry

    lax.fori_loop(0, NPART, pair_merge, 0)

    for d in FAR:
        to = (y + d) % NY
        src = rsa.at[to % NC, :, pl.ds(pl.multiple_of((to // NC) * (D // NH), D // NH), D // NH)]
        send(f"ya{d}", src, ra1.at[d], ra1.at[d], at_y(to))
        to = (z + d) % NZ
        send(f"zb{d}", rsb.at[to], rb1.at[d], rb1.at[d], at_z(to))
    send("q1hi", q.at[0, hi, :], q.at[1, hi, :], q.at[1, hi, :], at_x(right))
    send("q2lo", q.at[0, lo, :], q.at[2, lo, :], q.at[2, lo, :], at_x(left))
    for d in range(1, NY):
        arrived(f"cy{d}")
    ring_y = merge(sty, NY)
    put(styz, z, *ring_y)
    for d in FAR:
        send(f"cyz{d}", styz.at[z], styz.at[z], styz.at[(z + NZ - d) % NZ], at_z((z + d) % NZ))
    for d in range(1, NZ):
        arrived(f"cz{d}")
    ring_z = merge(stz, NZ)
    put(stzy, y, *ring_z)
    for d in FAR:
        send(f"czy{d}", stzy.at[y], stzy.at[y], stzy.at[(y + NY - d) % NY], at_y((y + d) % NY))
    turn([relative(sty, (y + NY - d) % NY, ring_y[0]) for d in range(NY)], col1a)
    turn([relative(stz, (z + NZ - d) % NZ, ring_z[0]) for d in range(NZ)], col1b)

    arrived("q1lo")
    send("q3lo", q.at[1, lo, :], q.at[3, lo, :], q.at[3, lo, :], at_x(right))
    arrived("q2hi")
    send("q3hi", q.at[2, hi, :], q.at[3, hi, :], q.at[3, hi, :], at_x(left))
    own = rsl[z].astype(F32)
    for d in range(1, NZ):
        arrived(f"zl{d}")
        own = own + rl1[d].astype(F32)
    rl2s[...] = own.astype(BF16)
    for d in FAR:
        to = (y + d) % NY
        src = rl2s.at[pl.ds(pl.multiple_of((to // NC) * (NC * HALF) + (to % NC) * HALF, HALF), HALF), :]
        send(f"yl{d}", src, rl2.at[d], rl2.at[d], at_y(to))

    for i, number in ((3, c), (0, from_block[0]), (1, from_block[1]), (2, from_block[2])):
        for d in (1, 3, 2):
            arrived(f"h{i}{d}")
            piece = hc.at[place[d], half_rows(number, k), :]
            send(f"g{i}{d}", piece, piece, hc.at[place[d], half_rows(number, 1 - k), :], partner)
    hc[0] = win[:, pl.ds(pl.multiple_of(x * COLS, COLS), COLS)]

    settle(("q", "ya", "zb", "cyz", "czy", "yl", "g"))
    rows_a = pl.ds(pl.multiple_of(c * TOK + k * HALF, QTR), QTR)
    rows_b = pl.ds(pl.multiple_of(c * TOK + k * HALF + QTR, QTR), QTR)
    factors = col1a[rows_a, :]
    own = rsa[c, :, pl.ds(pl.multiple_of(h * (D // NH), D // NH), D // NH)].astype(F32) * factors[:, 0:1]
    for d in range(1, NY):
        arrived(f"ya{d}")
        own = own + ra1[d].astype(F32) * factors[:, d : d + 1]
    ra2s[...] = own.astype(BF16)
    for d in FAR:
        to = (z + d) % NZ
        src = ra2s.at[:, pl.ds(pl.multiple_of(to * 128, 128), 128)]
        send(f"za{d}", src, ra2.at[d], ra2.at[d], at_z(to))
    factors = [
        col1b[pl.ds(pl.multiple_of(j * TOK + k * HALF + QTR, QTR), QTR), :] for j in range(NC)
    ]
    factors = jnp.concatenate(factors + factors, axis=0)
    own = rsb[z].astype(F32) * factors[:, 0:1]
    for d in range(1, NZ):
        arrived(f"zb{d}")
        own = own + rb1[d].astype(F32) * factors[:, d : d + 1]
    rb2s[...] = own.astype(BF16)
    for d in FAR:
        to = (y + d) % NY
        src = rb2s.at[pl.ds(pl.multiple_of((to // NC) * TOK + (to % NC) * QTR, QTR), QTR), :]
        send(f"yb{d}", src, rb2.at[d], rb2.at[d], at_y(to))
    settle(("q", "za", "yb"))
    for d in range(1, NZ):
        arrived(f"cyz{d}")
    all_top, all_rest, all_label = merge(styz, NZ)
    peak = jnp.maximum(all_top, all_label)
    rest = all_rest * jnp.exp(all_top - peak)
    whole = rest + jnp.exp(all_label - peak)
    log_total = peak + jnp.log(whole)
    row_total = unfold(log_total)
    coeff = token_weights(
        unfold(all_label - log_total), mask_ref[...], seq_ref[...], old_ref[...], refp_ref[...], adv_ref
    )
    factor = coeff * jnp.exp(top - row_total)
    label_grad = coeff * unfold(rest / whole)
    put(scale, 0, fold(factor), fold(label_grad), fold(label_grad))
    for d in (1, 3, 2):
        send(f"x{d}", scale.at[0], scale.at[d], scale.at[d], at_x((x + d) % NX))

    def form(slot, factor_row, label_row):
        def step(i, carry):
            part = q[slot, rows_of(i), :].astype(F32)
            grad = jnp.where(part < 0.0, label_row, -part * factor_row)
            gt[rows_of(i), slot * WIN : (slot + 1) * WIN] = grad.astype(BF16)
            return carry

        lax.fori_loop(0, ROWS // CH, step, 0)

    def rows_for(d):
        arrived(f"x{d}")
        return unfold(scale[d, 0:2, :]), unfold(scale[d, 2:4, :])

    form(0, factor, label_grad)
    for d in range(1, NY):
        arrived(f"czy{d}")
    turn([-coeff * relative(styz, (z + NZ - d) % NZ, log_total) for d in range(NZ)], col2a)
    turn([-coeff * relative(stzy, (y + NY - d) % NY, log_total) for d in range(NY)], col2b)
    turn([label_grad], coll)
    own = rl2s[pl.ds(pl.multiple_of(h * (NC * HALF) + c * HALF, HALF), HALF), :].astype(F32)
    for d in range(1, NY):
        arrived(f"yl{d}")
        own = own + rl2[d].astype(F32)
    own_label = own * coll[half_rows(c, k), :][:, 0:1]

    factors = col2a[rows_a, :]
    own = own_label[:QTR]
    own = own + ra2s[:, pl.ds(pl.multiple_of(z * 128, 128), 128)].astype(F32) * factors[:, 0:1]
    for d in range(1, NZ):
        arrived(f"za{d}")
        own = own + ra2[d].astype(F32) * factors[:, d : d + 1]
    fin[0, 0:QTR, :] = own.astype(BF16)
    factors = col2b[rows_b, :]
    own = own_label[QTR:]
    own = own + rb2s[pl.ds(pl.multiple_of(h * TOK + c * QTR, QTR), QTR), :].astype(F32) * factors[:, 0:1]
    for d in range(1, NY):
        arrived(f"yb{d}")
        own = own + rb2[d].astype(F32) * factors[:, d : d + 1]
    fin[0, QTR:HALF, :] = own.astype(BF16)
    send("fin", fin.at[0], fin.at[1], fin.at[1], partner)
    for i in range(4):
        for d in (1, 3, 2):
            arrived(f"g{i}{d}")
    near = rows_for(1)
    arrived("q1hi")
    form(1, *near)
    near = rows_for(3)
    arrived("q2lo")
    form(2, *near)

    across = rows_for(2)
    arrived("q3lo")
    arrived("q3hi")
    form(3, *across)

    def head_step(i, carry):
        head_ref[block_rows(i), :] = jnp.dot(
            gt[block_rows(i), :], hc[...].reshape(NX * WIN, COLS), preferred_element_type=F32
        ).astype(BF16)
        return carry

    lax.fori_loop(0, ROWS // BLOCK, head_step, 0)

    arrived("fin")
    for slot, row in ((0, k), (1, 1 - k)):
        value = fin[slot].astype(F32)
        value = jnp.where(k == 0, value[:, :64], value[:, 64:])
        hg_ref[0, pl.ds(pl.multiple_of(row * HALF, HALF), HALF), :] = value.astype(BF16)
    drain()


def body(*args):
    vmem = pl.BlockSpec(memory_space=pltpu.VMEM)
    hbm = pl.BlockSpec(memory_space=pltpu.HBM)
    dma = pltpu.SemaphoreType.DMA
    args = [pltpu.with_memory_space_constraint(a, pltpu.HBM) for a in args]
    return pl.pallas_call(
        kernel,
        out_shape=(
            pltpu.VMEM((1, TOK, D // (NH * NZ * 2)), BF16),
            pltpu.VMEM((ROWS, COLS), BF16),
        ),
        in_specs=[hbm] * 8,
        out_specs=(vmem, vmem),
        scratch_shapes=[
            pltpu.VMEM((ROWS, D), BF16),
            pltpu.VMEM((WIN, D), BF16),
            pltpu.VMEM((NX, WIN, COLS), BF16),
            pltpu.VMEM((ROWS, WIN), F32),
            pltpu.VMEM((NX, ROWS, WIN), BF16),
            pltpu.VMEM((ROWS, NX * WIN), BF16),
            pltpu.VMEM((WIN, ROWS), BF16),
            pltpu.VMEM((WIN // 2, D), F32),
            pltpu.VMEM((WIN // 2, D), BF16),
            pltpu.VMEM((WIN // 2, D), BF16),
            pltpu.VMEM((WIN // 2, D), BF16),
            pltpu.VMEM((WIN // 2, D), BF16),
            pltpu.VMEM((WIN // 2, D), BF16),
            pltpu.VMEM((NC, QTR, D), BF16),
            pltpu.VMEM((NZ, NH * TOK, 128), BF16),
            pltpu.VMEM((NZ, NH * NC * HALF, 128), BF16),
            pltpu.VMEM((NY, QTR, D // NH), BF16),
            pltpu.VMEM((NZ, NH * TOK, 128), BF16),
            pltpu.VMEM((NZ, NH * NC * HALF, 128), BF16),
            pltpu.VMEM((QTR, D // NH), BF16),
            pltpu.VMEM((NH * TOK, 128), BF16),
            pltpu.VMEM((NH * NC * HALF, 128), BF16),
            pltpu.VMEM((NZ, QTR, 128), BF16),
            pltpu.VMEM((NY, QTR, 128), BF16),
            pltpu.VMEM((NY, HALF, 128), BF16),
            pltpu.VMEM((2, HALF, 128), BF16),
            pltpu.VMEM((2, 8, 128), F32),
            pltpu.VMEM((NY, 8, 128), F32),
            pltpu.VMEM((NZ, 8, 128), F32),
            pltpu.VMEM((NZ, 8, 128), F32),
            pltpu.VMEM((NY, 8, 128), F32),
            pltpu.VMEM((NX, 8, 128), F32),
            pltpu.VMEM((WIN, 8), F32),
            pltpu.VMEM((WIN, 8), F32),
            pltpu.VMEM((WIN, 8), F32),
            pltpu.VMEM((WIN, 8), F32),
            pltpu.VMEM((WIN, 8), F32),
            pltpu.VMEM((WIN, 8), F32),
            pltpu.VMEM((1, WIN), jnp.int32),
            pltpu.VMEM((1, WIN), jnp.int32),
            pltpu.VMEM((1, WIN), jnp.int32),
            pltpu.VMEM((1, WIN), F32),
            pltpu.VMEM((1, WIN), F32),
            pltpu.VMEM((1, 8), F32),
            dma((8,)),
            dma((SEMS,)),
            dma((SEMS,)),
        ],
        compiler_params=pltpu.CompilerParams(
            collective_id=0, has_side_effects=True, vmem_limit_bytes=48 * 1024 * 1024
        ),
        cost_estimate=pl.CostEstimate(
            flops=8 * WIN * D * ROWS, bytes_accessed=2 * ROWS * (D + COLS), transcendentals=4 * ROWS * WIN
        ),
    )(*args)


def solution(mesh):
    placed = (P("dp", "ctx", None), P(("ctx", "vocab"), None)) + (P("dp", None),) * 6
    return jax.shard_map(
        body,
        mesh=mesh,
        in_specs=placed,
        out_specs=(P("dp", "ctx", "vocab"), P(("ctx", "vocab"), "dp")),
        check_vma=False,
    )
```

```python
import functools

import jax
import jax.numpy as jnp
from jax import lax
from jax.experimental import pallas as pl
from jax.experimental.pallas import tpu as pltpu
from jax.sharding import PartitionSpec as P

CLIP_LOW = 0.2
CLIP_HIGH = 0.28
DUAL_CLIP = 3.0
KL_COEF = 0.04
KL_CAP = 10.0
LOSS_SCALE = 64.0

MESH = pl.DeviceIdType.MESH
F32 = jnp.float32
BF16 = jnp.bfloat16

NX = 4
NC = 4
NH = 2
NY = NC * NH
NZ = 8
WIN = 256
TOK = WIN // NC
HALF = TOK // 2
QTR = HALF // 2
D = 2048
ROWS = 896
CH = 128
COLS = D // NX
PART = 512
NPART = D // PART
SPLIT = ROWS // 2


def sequence_terms(seq, adv_ref):
    adv = jnp.zeros(seq.shape, F32)
    length = jnp.zeros(seq.shape, F32)
    for s in range(adv_ref.shape[1]):
        match = (seq == s).astype(F32)
        count = jnp.sum(match, axis=1, keepdims=True)
        adv = adv + match * adv_ref[0:1, s : s + 1]
        length = length + match * count
    return adv, length


def token_weights(logp, mask, adv, length, old, ref):
    ratio = jnp.exp(logp - old)
    low = jnp.where(ratio >= 1.0 - CLIP_LOW, jnp.where(ratio <= DUAL_CLIP, 1.0, 0.0), 0.0)
    active = jnp.where(adv >= 0.0, jnp.where(ratio <= 1.0 + CLIP_HIGH, 1.0, 0.0), low)
    policy = jnp.where(active > 0.0, -adv * ratio, 0.0)
    gap = ref - logp
    exp_gap = jnp.exp(gap)
    penalty = jnp.where(exp_gap - gap - 1.0 < KL_CAP, 1.0 - exp_gap, 0.0)
    return LOSS_SCALE * mask.astype(F32) * (policy + KL_COEF * penalty) / length


def merge(ref, n):
    top = ref[0, 0:2, :]
    for i in range(1, n):
        top = jnp.maximum(top, ref[i, 0:2, :])
    total = jnp.zeros_like(top)
    label = jnp.zeros_like(top)
    for i in range(n):
        total = total + ref[i, 2:4, :] * jnp.exp(ref[i, 0:2, :] - top)
        label = label + ref[i, 4:6, :]
    return top, total, label


def turn(rows, out):
    rows = list(rows) + [jnp.zeros_like(rows[0])] * (8 - len(rows))
    out[...] = jnp.concatenate(rows, axis=0).T


def put(ref, slot, top, total, label):
    ref[slot] = jnp.concatenate([top, total, label, jnp.zeros_like(top)], axis=0)


def fold(row):
    return jnp.concatenate([row[:, :128], row[:, 128:]], axis=0)


def unfold(tile):
    return jnp.concatenate([tile[0:1, :], tile[1:2, :]], axis=1)


SEMS = 160
BLOCK = 448
FAR = (4, 3, 5, 2, 6, 1, 7)


def kernel(
    hid_hbm,
    w_hbm,
    lab_hbm,
    mask_hbm,
    seq_hbm,
    old_hbm,
    refp_hbm,
    adv_hbm,
    hg_ref,
    head_ref,
    w,
    win,
    hc,
    logit,
    q,
    gt,
    g,
    keep,
    e1s,
    e1r,
    keepl,
    els,
    elr,
    rsa,
    rsb,
    rsl,
    rsla,
    ra1,
    rb1,
    rl1,
    rk1,
    ra2s,
    rb2s,
    rl2s,
    rk2s,
    ra2,
    rb2,
    rl2,
    rk2,
    fin,
    st0,
    sty,
    stz,
    styz,
    stzy,
    scale,
    col0,
    col1a,
    col1b,
    col2a,
    col2b,
    coll,
    lab_ref,
    mask_ref,
    seq_ref,
    old_ref,
    refp_ref,
    adv_ref,
    loc_sem,
    send_sems,
    recv_sems,
):
    x = lax.axis_index("dp")
    c = lax.axis_index("ctx")
    v = lax.axis_index("vocab")
    h = v // (NZ * 2)
    z = (v // 2) % NZ
    k = v % 2
    y = h * NC + c

    def at_y(to):
        return (x, to % NC, (to // NC) * (NZ * 2) + z * 2 + k)

    def at_z(to):
        return (x, c, h * (NZ * 2) + to * 2 + k)

    def at_x(to):
        return (to, c, v)

    partner = (x, c, h * (NZ * 2) + z * 2 + (1 - k))

    sent = []
    coming = {}
    names = []
    settled = set()

    def send(name, src, dst, landing, to):
        at = len(sent)
        copy = pltpu.make_async_remote_copy(
            src_ref=src,
            dst_ref=dst,
            send_sem=send_sems.at[at],
            recv_sem=recv_sems.at[at],
            device_id=to,
            device_id_type=MESH,
        )
        copy.start()
        sent.append(copy)
        names.append(name)
        coming[name] = pltpu.make_async_remote_copy(
            src_ref=landing,
            dst_ref=landing,
            send_sem=send_sems.at[at],
            recv_sem=recv_sems.at[at],
            device_id=to,
            device_id_type=MESH,
        )

    def arrived(name):
        coming.pop(name).wait_recv()

    def drain():
        for name in list(coming):
            arrived(name)
        settle(())

    def settle(later):
        for at, copy in enumerate(sent):
            if at not in settled and not (later and names[at].startswith(later)):
                copy.wait_send()
                settled.add(at)

    block = pl.ds(pl.multiple_of(c * TOK, TOK), TOK)
    load_hid = pltpu.make_async_copy(hid_hbm.at[0], win.at[block, :], loc_sem.at[0])
    load_hid.start()
    load_w = pltpu.make_async_copy(w_hbm, w, loc_sem.at[1])
    load_w.start()
    loads = []
    for i, (src, dst) in enumerate(
        (
            (lab_hbm, lab_ref),
            (mask_hbm, mask_ref),
            (seq_hbm, seq_ref),
            (old_hbm, old_ref),
            (refp_hbm, refp_ref),
            (adv_hbm, adv_ref),
        )
    ):
        loads.append(pltpu.make_async_copy(src, dst, loc_sem.at[2 + i]))
        loads[-1].start()

    barrier = pltpu.get_barrier_semaphore()
    peers = [partner]
    peers += [at_y((y + d) % NY) for d in range(1, NY)]
    peers += [at_z((z + d) % NZ) for d in range(1, NZ)]
    peers += [at_x((x + d) % NX) for d in range(1, NX)]
    for peer in peers:
        pl.semaphore_signal(barrier, inc=1, device_id=peer, device_id_type=MESH)
    pl.semaphore_wait(barrier, len(peers))

    def half_rows(number, half):
        return pl.ds(pl.multiple_of(number * TOK + half * HALF, HALF), HALF)

    def rows_of(i):
        return pl.ds(pl.multiple_of(i * CH, CH), CH)

    place = {0: 0, 1: 1, 3: 2, 2: 3}
    right, left = (x + 1) % NX, (x + NX - 1) % NX

    far = (y + NY + 2 - 4 * k) % NY
    from_block = ((c + NC - 1) % NC, (c + 1) % NC, (c + 2) % NC)
    mine = hid_hbm.at[0, pl.ds(pl.multiple_of(k * HALF, HALF), HALF), :]
    for i, to in ((2, far), (0, (y + 1) % NY), (1, (y + NY - 1) % NY)):
        send(
            f"a{i}", mine, win.at[half_rows(c, k), :], win.at[half_rows(from_block[i], k), :], at_y(to)
        )

    def spread_columns(i, number, src):
        for d in (1, 3, 2):
            to = (x + d) % NX
            part = src.at[:, pl.ds(pl.multiple_of(to * COLS, COLS), COLS)]
            dst = hc.at[place[d], half_rows(number, k), :]
            send(f"h{i}{d}", part, dst, dst, at_x(to))

    spread_columns(3, c, mine)

    load_w.wait()
    for load in loads:
        load.wait()
    base = (c * (NH * NZ * 2) + v) * ROWS
    local_label = lab_ref[...] - base

    def hit(i):
        rows = lax.broadcasted_iota(jnp.int32, (CH, WIN), 0) + i * CH
        return rows == local_label

    def put_turned(i, value):
        turned = value.T.astype(BF16)
        for j in range(NC):
            for half in range(2):
                row = j * HALF + (WIN // 2) * (1 - k if half == 0 else k)
                start = j * TOK + half * HALF
                g[pl.ds(pl.multiple_of(row, HALF), HALF), rows_of(i)] = turned[start : start + HALF]

    def label_step(i, carry):
        put_turned(i, hit(i).astype(F32))
        return carry

    lax.fori_loop(0, ROWS // CH, label_step, 0)

    def part_cols(n):
        return pl.ds(pl.multiple_of(n * PART, PART), PART)

    def label_dot(n, carry):
        cols = part_cols(n)
        value = jnp.dot(g[...], w[:, cols], preferred_element_type=F32)
        els[:, cols] = value[: WIN // 2].astype(BF16)
        keepl[:, cols] = value[WIN // 2 :].astype(BF16)
        return carry

    lax.fori_loop(0, NPART, label_dot, 0)
    send("l", els, elr, elr, partner)
    arrived("l")

    def label_merge(j, carry):
        rows = pl.ds(pl.multiple_of(j * HALF, HALF), HALF)
        both = (keepl[rows, :].astype(F32) + elr[rows, :].astype(F32)).astype(BF16)
        rsla[j] = both[:QTR]
        for m in range(D // 128):
            hh, zz = m // NZ, m % NZ
            rows = pl.ds(pl.multiple_of(hh * TOK + j * QTR, QTR), QTR)
            rsl[zz, rows, :] = both[QTR:, m * 128 : (m + 1) * 128]
        return carry

    lax.fori_loop(0, NC, label_merge, 0)
    for d in FAR:
        to = (z + d) % NZ
        send(f"zl{d}", rsl.at[to], rl1.at[d], rl1.at[d], at_z(to))

    adv, length = sequence_terms(seq_ref[...], adv_ref)

    for i in range(3):
        arrived(f"a{i}")
        piece = win.at[half_rows(from_block[i], k), :]
        send(f"f{i}", piece, piece, win.at[half_rows(from_block[i], 1 - k), :], partner)
        spread_columns(i, from_block[i], piece)
    load_hid.wait()
    for i in range(3):
        arrived(f"f{i}")
    for d in FAR:
        to = (y + d) % NY
        src = rsla.at[to % NC, :, pl.ds(pl.multiple_of((to // NC) * (D // NH), D // NH), D // NH)]
        send(f"yk{d}", src, rk1.at[d], rk1.at[d], at_y(to))
    def block_rows(i):
        return pl.ds(pl.multiple_of(i * BLOCK, BLOCK), BLOCK)

    def logit_step(i, carry):
        logit[block_rows(i), :] = lax.dot_general(
            w[block_rows(i), :], win[...], (((1,), (1,)), ((), ())), preferred_element_type=F32
        )
        return carry

    lax.fori_loop(0, ROWS // BLOCK, logit_step, 0)

    def stat_step(i, carry):
        top, label = carry
        part = logit[rows_of(i), :]
        here = hit(i)
        top = jnp.maximum(top, jnp.max(jnp.where(here, -jnp.inf, part), axis=0, keepdims=True))
        label = label + jnp.sum(jnp.where(here, part, 0.0), axis=0, keepdims=True)
        return top, label

    top, label = lax.fori_loop(
        0, ROWS // CH, stat_step, (jnp.full((1, WIN), -jnp.inf, F32), jnp.zeros((1, WIN), F32))
    )

    def exp_step(i, total):
        here = hit(i)
        part = jnp.where(here, 0.0, jnp.exp(logit[rows_of(i), :] - top))
        q[0, rows_of(i), :] = jnp.where(here, -1.0, part).astype(BF16)
        put_turned(i, part)
        return total + jnp.sum(part, axis=0, keepdims=True)

    total = lax.fori_loop(0, ROWS // CH, exp_step, jnp.zeros((1, WIN), F32))
    put(st0, k, fold(top), fold(total), fold(label))
    send("c", st0.at[k], st0.at[k], st0.at[1 - k], partner)

    lo, hi = pl.ds(0, SPLIT), pl.ds(SPLIT, SPLIT)
    send("q1lo", q.at[0, lo, :], q.at[1, lo, :], q.at[1, lo, :], at_x(right))
    send("q2hi", q.at[0, hi, :], q.at[2, hi, :], q.at[2, hi, :], at_x(left))
    first = len(sent)

    def swap(n):
        return pltpu.make_async_remote_copy(
            src_ref=e1s.at[:, part_cols(n)],
            dst_ref=e1r.at[:, part_cols(n)],
            send_sem=send_sems.at[first + n],
            recv_sem=recv_sems.at[first + n],
            device_id=partner,
            device_id_type=MESH,
        )

    def weight_sums(n, carry):
        cols = part_cols(n)
        value = jnp.dot(g[...], w[:, cols], preferred_element_type=F32)
        e1s[:, cols] = value[: WIN // 2].astype(BF16)
        keep[:, cols] = value[WIN // 2 :]
        swap(n).start()
        return carry

    lax.fori_loop(0, NPART, weight_sums, 0)
    sent.extend(swap(n) for n in range(NPART))
    names.extend("e" for n in range(NPART))

    arrived("c")
    pair = merge(st0, 2)
    put(sty, y, *pair)
    put(stz, z, *pair)
    for d in FAR:
        send(f"cy{d}", sty.at[y], sty.at[y], sty.at[(y + NY - d) % NY], at_y((y + d) % NY))
    for d in FAR:
        send(f"cz{d}", stz.at[z], stz.at[z], stz.at[(z + NZ - d) % NZ], at_z((z + d) % NZ))

    def relative(ref, slot, norm):
        return unfold(jnp.exp(ref[slot, 0:2, :] - norm))

    turn([relative(st0, k, pair[0]), relative(st0, 1 - k, pair[0])], col0)

    def pair_merge(n, carry):
        cols = part_cols(n)
        swap(n).wait_recv()
        for j in range(NC):
            rows = slice(j * HALF, (j + 1) * HALF)
            factors = col0[half_rows(j, k), :]
            both = keep[rows, cols] * factors[:, 0:1] + e1r[rows, cols].astype(F32) * factors[:, 1:2]
            both = both.astype(BF16)
            rsa[j, :, cols] = both[:QTR]
            for m in range(PART // 128):
                hh, zz = n // (NPART // NH), n % (NPART // NH) * (PART // 128) + m
                rows_b = pl.ds(pl.multiple_of(hh * TOK + j * QTR, QTR), QTR)
                rsb[zz, rows_b, :] = both[QTR:, m * 128 : (m + 1) * 128]
        return carry

    lax.fori_loop(0, NPART, pair_merge, 0)

    for d in FAR:
        to = (y + d) % NY
        src = rsa.at[to % NC, :, pl.ds(pl.multiple_of((to // NC) * (D // NH), D // NH), D // NH)]
        send(f"ya{d}", src, ra1.at[d], ra1.at[d], at_y(to))
        to = (z + d) % NZ
        send(f"zb{d}", rsb.at[to], rb1.at[d], rb1.at[d], at_z(to))
    send("q1hi", q.at[0, hi, :], q.at[1, hi, :], q.at[1, hi, :], at_x(right))
    send("q2lo", q.at[0, lo, :], q.at[2, lo, :], q.at[2, lo, :], at_x(left))
    for d in range(1, NY):
        arrived(f"cy{d}")
    ring_y = merge(sty, NY)
    put(styz, z, *ring_y)
    for d in FAR:
        send(f"cyz{d}", styz.at[z], styz.at[z], styz.at[(z + NZ - d) % NZ], at_z((z + d) % NZ))
    for d in range(1, NZ):
        arrived(f"cz{d}")
    ring_z = merge(stz, NZ)
    put(stzy, y, *ring_z)
    for d in FAR:
        send(f"czy{d}", stzy.at[y], stzy.at[y], stzy.at[(y + NY - d) % NY], at_y((y + d) % NY))
    turn([relative(sty, (y + NY - d) % NY, ring_y[0]) for d in range(NY)], col1a)
    turn([relative(stz, (z + NZ - d) % NZ, ring_z[0]) for d in range(NZ)], col1b)

    arrived("q1lo")
    send("q3lo", q.at[1, lo, :], q.at[3, lo, :], q.at[3, lo, :], at_x(right))
    arrived("q2hi")
    send("q3hi", q.at[2, hi, :], q.at[3, hi, :], q.at[3, hi, :], at_x(left))
    own = rsl[z].astype(F32)
    for d in range(1, NZ):
        arrived(f"zl{d}")
        own = own + rl1[d].astype(F32)
    rl2s[...] = own.astype(BF16)
    for d in FAR:
        to = (y + d) % NY
        src = rl2s.at[pl.ds(pl.multiple_of((to // NC) * TOK + (to % NC) * QTR, QTR), QTR), :]
        send(f"yl{d}", src, rl2.at[d], rl2.at[d], at_y(to))
    own = rsla[c, :, pl.ds(pl.multiple_of(h * (D // NH), D // NH), D // NH)].astype(F32)
    for d in range(1, NY):
        arrived(f"yk{d}")
        own = own + rk1[d].astype(F32)
    rk2s[...] = own.astype(BF16)
    for d in FAR:
        to = (z + d) % NZ
        src = rk2s.at[:, pl.ds(pl.multiple_of(to * 128, 128), 128)]
        send(f"zk{d}", src, rk2.at[d], rk2.at[d], at_z(to))

    for i, number in ((3, c), (0, from_block[0]), (1, from_block[1]), (2, from_block[2])):
        for d in (1, 3, 2):
            arrived(f"h{i}{d}")
            piece = hc.at[place[d], half_rows(number, k), :]
            send(f"g{i}{d}", piece, piece, hc.at[place[d], half_rows(number, 1 - k), :], partner)
    hc[0] = win[:, pl.ds(pl.multiple_of(x * COLS, COLS), COLS)]

    settle(("q", "ya", "zb", "cyz", "czy", "yl", "zk", "g"))
    rows_a = pl.ds(pl.multiple_of(c * TOK + k * HALF, QTR), QTR)
    rows_b = pl.ds(pl.multiple_of(c * TOK + k * HALF + QTR, QTR), QTR)
    factors = col1a[rows_a, :]
    own = rsa[c, :, pl.ds(pl.multiple_of(h * (D // NH), D // NH), D // NH)].astype(F32) * factors[:, 0:1]
    for d in range(1, NY):
        arrived(f"ya{d}")
        own = own + ra1[d].astype(F32) * factors[:, d : d + 1]
    ra2s[...] = own.astype(BF16)
    for d in FAR:
        to = (z + d) % NZ
        src = ra2s.at[:, pl.ds(pl.multiple_of(to * 128, 128), 128)]
        send(f"za{d}", src, ra2.at[d], ra2.at[d], at_z(to))
    factors = [
        col1b[pl.ds(pl.multiple_of(j * TOK + k * HALF + QTR, QTR), QTR), :] for j in range(NC)
    ]
    factors = jnp.concatenate(factors + factors, axis=0)
    own = rsb[z].astype(F32) * factors[:, 0:1]
    for d in range(1, NZ):
        arrived(f"zb{d}")
        own = own + rb1[d].astype(F32) * factors[:, d : d + 1]
    rb2s[...] = own.astype(BF16)
    for d in FAR:
        to = (y + d) % NY
        src = rb2s.at[pl.ds(pl.multiple_of((to // NC) * TOK + (to % NC) * QTR, QTR), QTR), :]
        send(f"yb{d}", src, rb2.at[d], rb2.at[d], at_y(to))
    settle(("q", "za", "yb"))
    for d in range(1, NZ):
        arrived(f"cyz{d}")
    all_top, all_rest, all_label = merge(styz, NZ)
    peak = jnp.maximum(all_top, all_label)
    rest = all_rest * jnp.exp(all_top - peak)
    whole = rest + jnp.exp(all_label - peak)
    log_total = peak + jnp.log(whole)
    row_total = unfold(log_total)
    coeff = token_weights(
        unfold(all_label - log_total), mask_ref[...], adv, length, old_ref[...], refp_ref[...]
    )
    factor = coeff * jnp.exp(top - row_total)
    label_grad = coeff * unfold(rest / whole)
    put(scale, 0, fold(factor), fold(label_grad), fold(label_grad))
    for d in (1, 3, 2):
        send(f"x{d}", scale.at[0], scale.at[d], scale.at[d], at_x((x + d) % NX))

    def form(slot, factor_row, label_row):
        def step(i, carry):
            part = q[slot, rows_of(i), :].astype(F32)
            grad = jnp.where(part < 0.0, label_row, -part * factor_row)
            gt[rows_of(i), slot * WIN : (slot + 1) * WIN] = grad.astype(BF16)
            return carry

        lax.fori_loop(0, ROWS // CH, step, 0)

    def rows_for(d):
        arrived(f"x{d}")
        return unfold(scale[d, 0:2, :]), unfold(scale[d, 2:4, :])

    form(0, factor, label_grad)
    for d in range(1, NY):
        arrived(f"czy{d}")
    turn([-coeff * relative(styz, (z + NZ - d) % NZ, log_total) for d in range(NZ)], col2a)
    turn([-coeff * relative(stzy, (y + NY - d) % NY, log_total) for d in range(NY)], col2b)
    turn([label_grad], coll)
    own = rk2s[:, pl.ds(pl.multiple_of(z * 128, 128), 128)].astype(F32)
    for d in range(1, NZ):
        arrived(f"zk{d}")
        own = own + rk2[d].astype(F32)
    other = rl2s[pl.ds(pl.multiple_of(h * TOK + c * QTR, QTR), QTR), :].astype(F32)
    for d in range(1, NY):
        arrived(f"yl{d}")
        other = other + rl2[d].astype(F32)
    own_label = jnp.concatenate([own, other], axis=0) * coll[half_rows(c, k), :][:, 0:1]

    factors = col2a[rows_a, :]
    own = own_label[:QTR]
    own = own + ra2s[:, pl.ds(pl.multiple_of(z * 128, 128), 128)].astype(F32) * factors[:, 0:1]
    for d in range(1, NZ):
        arrived(f"za{d}")
        own = own + ra2[d].astype(F32) * factors[:, d : d + 1]
    fin[0, 0:QTR, :] = own.astype(BF16)
    factors = col2b[rows_b, :]
    own = own_label[QTR:]
    own = own + rb2s[pl.ds(pl.multiple_of(h * TOK + c * QTR, QTR), QTR), :].astype(F32) * factors[:, 0:1]
    for d in range(1, NY):
        arrived(f"yb{d}")
        own = own + rb2[d].astype(F32) * factors[:, d : d + 1]
    fin[0, QTR:HALF, :] = own.astype(BF16)
    send("fin", fin.at[0], fin.at[1], fin.at[1], partner)
    for i in range(4):
        for d in (1, 3, 2):
            arrived(f"g{i}{d}")
    near = rows_for(1)
    arrived("q1hi")
    form(1, *near)
    near = rows_for(3)
    arrived("q2lo")
    form(2, *near)

    across = rows_for(2)
    arrived("q3lo")
    arrived("q3hi")
    form(3, *across)

    def head_step(i, carry):
        head_ref[block_rows(i), :] = jnp.dot(
            gt[block_rows(i), :], hc[...].reshape(NX * WIN, COLS), preferred_element_type=F32
        ).astype(BF16)
        return carry

    lax.fori_loop(0, ROWS // BLOCK, head_step, 0)

    arrived("fin")
    for slot, row in ((0, k), (1, 1 - k)):
        value = fin[slot].astype(F32)
        value = jnp.where(k == 0, value[:, :64], value[:, 64:])
        hg_ref[0, pl.ds(pl.multiple_of(row * HALF, HALF), HALF), :] = value.astype(BF16)
    drain()


def body(*args):
    vmem = pl.BlockSpec(memory_space=pltpu.VMEM)
    hbm = pl.BlockSpec(memory_space=pltpu.HBM)
    dma = pltpu.SemaphoreType.DMA
    args = [pltpu.with_memory_space_constraint(a, pltpu.HBM) for a in args]
    return pl.pallas_call(
        kernel,
        out_shape=(
            pltpu.VMEM((1, TOK, D // (NH * NZ * 2)), BF16),
            pltpu.VMEM((ROWS, COLS), BF16),
        ),
        in_specs=[hbm] * 8,
        out_specs=(vmem, vmem),
        scratch_shapes=[
            pltpu.VMEM((ROWS, D), BF16),
            pltpu.VMEM((WIN, D), BF16),
            pltpu.VMEM((NX, WIN, COLS), BF16),
            pltpu.VMEM((ROWS, WIN), F32),
            pltpu.VMEM((NX, ROWS, WIN), BF16),
            pltpu.VMEM((ROWS, NX * WIN), BF16),
            pltpu.VMEM((WIN, ROWS), BF16),
            pltpu.VMEM((WIN // 2, D), F32),
            pltpu.VMEM((WIN // 2, D), BF16),
            pltpu.VMEM((WIN // 2, D), BF16),
            pltpu.VMEM((WIN // 2, D), BF16),
            pltpu.VMEM((WIN // 2, D), BF16),
            pltpu.VMEM((WIN // 2, D), BF16),
            pltpu.VMEM((NC, QTR, D), BF16),
            pltpu.VMEM((NZ, NH * TOK, 128), BF16),
            pltpu.VMEM((NZ, NH * TOK, 128), BF16),
            pltpu.VMEM((NC, QTR, D), BF16),
            pltpu.VMEM((NY, QTR, D // NH), BF16),
            pltpu.VMEM((NZ, NH * TOK, 128), BF16),
            pltpu.VMEM((NZ, NH * TOK, 128), BF16),
            pltpu.VMEM((NY, QTR, D // NH), BF16),
            pltpu.VMEM((QTR, D // NH), BF16),
            pltpu.VMEM((NH * TOK, 128), BF16),
            pltpu.VMEM((NH * TOK, 128), BF16),
            pltpu.VMEM((QTR, D // NH), BF16),
            pltpu.VMEM((NZ, QTR, 128), BF16),
            pltpu.VMEM((NY, QTR, 128), BF16),
            pltpu.VMEM((NY, QTR, 128), BF16),
            pltpu.VMEM((NZ, QTR, 128), BF16),
            pltpu.VMEM((2, HALF, 128), BF16),
            pltpu.VMEM((2, 8, 128), F32),
            pltpu.VMEM((NY, 8, 128), F32),
            pltpu.VMEM((NZ, 8, 128), F32),
            pltpu.VMEM((NZ, 8, 128), F32),
            pltpu.VMEM((NY, 8, 128), F32),
            pltpu.VMEM((NX, 8, 128), F32),
            pltpu.VMEM((WIN, 8), F32),
            pltpu.VMEM((WIN, 8), F32),
            pltpu.VMEM((WIN, 8), F32),
            pltpu.VMEM((WIN, 8), F32),
            pltpu.VMEM((WIN, 8), F32),
            pltpu.VMEM((WIN, 8), F32),
            pltpu.VMEM((1, WIN), jnp.int32),
            pltpu.VMEM((1, WIN), jnp.int32),
            pltpu.VMEM((1, WIN), jnp.int32),
            pltpu.VMEM((1, WIN), F32),
            pltpu.VMEM((1, WIN), F32),
            pltpu.VMEM((1, 8), F32),
            dma((8,)),
            dma((SEMS,)),
            dma((SEMS,)),
        ],
        compiler_params=pltpu.CompilerParams(
            collective_id=0, has_side_effects=True, vmem_limit_bytes=48 * 1024 * 1024
        ),
        cost_estimate=pl.CostEstimate(
            flops=8 * WIN * D * ROWS, bytes_accessed=2 * ROWS * (D + COLS), transcendentals=4 * ROWS * WIN
        ),
    )(*args)


def solution(mesh):
    placed = (P("dp", "ctx", None), P(("ctx", "vocab"), None)) + (P("dp", None),) * 6
    return jax.shard_map(
        body,
        mesh=mesh,
        in_specs=placed,
        out_specs=(P("dp", "ctx", "vocab"), P(("ctx", "vocab"), "dp")),
        check_vma=False,
    )
```

```python
import functools

import jax
import jax.numpy as jnp
from jax import lax
from jax.experimental import pallas as pl
from jax.experimental.pallas import tpu as pltpu
from jax.sharding import PartitionSpec as P

CLIP_LOW = 0.2
CLIP_HIGH = 0.28
DUAL_CLIP = 3.0
KL_COEF = 0.04
KL_CAP = 10.0
LOSS_SCALE = 64.0

MESH = pl.DeviceIdType.MESH
F32 = jnp.float32
BF16 = jnp.bfloat16

NX = 4
NC = 4
NH = 2
NY = NC * NH
NZ = 8
WIN = 256
TOK = WIN // NC
HALF = TOK // 2
QTR = HALF // 2
D = 2048
ROWS = 896
CH = 128
COLS = D // NX
PART = 512
NPART = D // PART
SPLIT = ROWS // 2


def sequence_terms(seq, adv_ref):
    adv = jnp.zeros(seq.shape, F32)
    length = jnp.zeros(seq.shape, F32)
    for s in range(adv_ref.shape[1]):
        match = (seq == s).astype(F32)
        count = jnp.sum(match, axis=1, keepdims=True)
        adv = adv + match * adv_ref[0:1, s : s + 1]
        length = length + match * count
    return adv, length


def token_weights(logp, mask, adv, length, old, ref):
    ratio = jnp.exp(logp - old)
    low = jnp.where(ratio >= 1.0 - CLIP_LOW, jnp.where(ratio <= DUAL_CLIP, 1.0, 0.0), 0.0)
    active = jnp.where(adv >= 0.0, jnp.where(ratio <= 1.0 + CLIP_HIGH, 1.0, 0.0), low)
    policy = jnp.where(active > 0.0, -adv * ratio, 0.0)
    gap = ref - logp
    exp_gap = jnp.exp(gap)
    penalty = jnp.where(exp_gap - gap - 1.0 < KL_CAP, 1.0 - exp_gap, 0.0)
    return LOSS_SCALE * mask.astype(F32) * (policy + KL_COEF * penalty) / length


def merge(ref, n):
    top = ref[0, 0:2, :]
    for i in range(1, n):
        top = jnp.maximum(top, ref[i, 0:2, :])
    total = jnp.zeros_like(top)
    label = jnp.zeros_like(top)
    for i in range(n):
        total = total + ref[i, 2:4, :] * jnp.exp(ref[i, 0:2, :] - top)
        label = label + ref[i, 4:6, :]
    return top, total, label


def turn(rows, out):
    rows = list(rows) + [jnp.zeros_like(rows[0])] * (8 - len(rows))
    out[...] = jnp.concatenate(rows, axis=0).T


def put(ref, slot, top, total, label):
    ref[slot] = jnp.concatenate([top, total, label, jnp.zeros_like(top)], axis=0)


def fold(row):
    return jnp.concatenate([row[:, :128], row[:, 128:]], axis=0)


def unfold(tile):
    return jnp.concatenate([tile[0:1, :], tile[1:2, :]], axis=1)


SEMS = 160
BLOCK = 448
FAR = (4, 3, 5, 2, 6, 1, 7)


def kernel(
    hid_hbm,
    w_hbm,
    lab_hbm,
    mask_hbm,
    seq_hbm,
    old_hbm,
    refp_hbm,
    adv_hbm,
    hg_ref,
    head_ref,
    w,
    win,
    hc,
    logit,
    q,
    gt,
    g,
    keep,
    e1s,
    e1r,
    keepl,
    els,
    elr,
    rsa,
    rsb,
    rsl,
    rsla,
    ra1,
    rb1,
    rl1,
    rk1,
    ra2s,
    rb2s,
    rl2s,
    rk2s,
    ra2,
    rb2,
    rl2,
    rk2,
    fin,
    st0,
    sty,
    stz,
    styz,
    stzy,
    scale,
    col0,
    col1a,
    col1b,
    col2a,
    col2b,
    coll,
    lab_ref,
    mask_ref,
    seq_ref,
    old_ref,
    refp_ref,
    adv_ref,
    loc_sem,
    send_sems,
    recv_sems,
):
    x = lax.axis_index("dp")
    c = lax.axis_index("ctx")
    v = lax.axis_index("vocab")
    h = v // (NZ * 2)
    z = (v // 2) % NZ
    k = v % 2
    y = h * NC + c

    def at_y(to):
        return (x, to % NC, (to // NC) * (NZ * 2) + z * 2 + k)

    def at_z(to):
        return (x, c, h * (NZ * 2) + to * 2 + k)

    def at_x(to):
        return (to, c, v)

    partner = (x, c, h * (NZ * 2) + z * 2 + (1 - k))

    sent = []
    coming = {}
    names = []
    settled = set()

    def send(name, src, dst, landing, to):
        at = len(sent)
        copy = pltpu.make_async_remote_copy(
            src_ref=src,
            dst_ref=dst,
            send_sem=send_sems.at[at],
            recv_sem=recv_sems.at[at],
            device_id=to,
            device_id_type=MESH,
        )
        copy.start()
        sent.append(copy)
        names.append(name)
        coming[name] = pltpu.make_async_remote_copy(
            src_ref=landing,
            dst_ref=landing,
            send_sem=send_sems.at[at],
            recv_sem=recv_sems.at[at],
            device_id=to,
            device_id_type=MESH,
        )

    def arrived(name):
        coming.pop(name).wait_recv()

    def drain():
        for name in list(coming):
            arrived(name)
        settle(())

    def settle(later):
        for at, copy in enumerate(sent):
            if at not in settled and not (later and names[at].startswith(later)):
                copy.wait_send()
                settled.add(at)

    block = pl.ds(pl.multiple_of(c * TOK, TOK), TOK)
    load_hid = pltpu.make_async_copy(hid_hbm.at[0], win.at[block, :], loc_sem.at[0])
    load_hid.start()
    load_w = pltpu.make_async_copy(w_hbm, w, loc_sem.at[1])
    load_w.start()
    loads = []
    for i, (src, dst) in enumerate(
        (
            (lab_hbm, lab_ref),
            (mask_hbm, mask_ref),
            (seq_hbm, seq_ref),
            (old_hbm, old_ref),
            (refp_hbm, refp_ref),
            (adv_hbm, adv_ref),
        )
    ):
        loads.append(pltpu.make_async_copy(src, dst, loc_sem.at[2 + i]))
        loads[-1].start()

    barrier = pltpu.get_barrier_semaphore()
    peers = [partner]
    peers += [at_y((y + d) % NY) for d in range(1, NY)]
    peers += [at_z((z + d) % NZ) for d in range(1, NZ)]
    peers += [at_x((x + d) % NX) for d in range(1, NX)]
    for peer in peers:
        pl.semaphore_signal(barrier, inc=1, device_id=peer, device_id_type=MESH)
    pl.semaphore_wait(barrier, len(peers))

    def half_rows(number, half):
        return pl.ds(pl.multiple_of(number * TOK + half * HALF, HALF), HALF)

    def rows_of(i):
        return pl.ds(pl.multiple_of(i * CH, CH), CH)

    place = {0: 0, 1: 1, 3: 2, 2: 3}
    right, left = (x + 1) % NX, (x + NX - 1) % NX

    far = (y + NY + 2 - 4 * k) % NY
    from_block = ((c + NC - 1) % NC, (c + 1) % NC, (c + 2) % NC)
    mine = hid_hbm.at[0, pl.ds(pl.multiple_of(k * HALF, HALF), HALF), :]
    for i, to in ((2, far), (0, (y + 1) % NY), (1, (y + NY - 1) % NY)):
        send(
            f"a{i}", mine, win.at[half_rows(c, k), :], win.at[half_rows(from_block[i], k), :], at_y(to)
        )

    def spread_columns(i, number, src):
        for d in (1, 3, 2):
            to = (x + d) % NX
            part = src.at[:, pl.ds(pl.multiple_of(to * COLS, COLS), COLS)]
            dst = hc.at[place[d], half_rows(number, k), :]
            send(f"h{i}{d}", part, dst, dst, at_x(to))

    spread_columns(3, c, mine)

    load_w.wait()
    for load in loads:
        load.wait()
    base = (c * (NH * NZ * 2) + v) * ROWS
    local_label = lab_ref[...] - base

    def hit(i):
        rows = lax.broadcasted_iota(jnp.int32, (CH, WIN), 0) + i * CH
        return rows == local_label

    def put_turned(i, value):
        turned = value.T.astype(BF16)
        for j in range(NC):
            for half in range(2):
                row = j * HALF + (WIN // 2) * (1 - k if half == 0 else k)
                start = j * TOK + half * HALF
                g[pl.ds(pl.multiple_of(row, HALF), HALF), rows_of(i)] = turned[start : start + HALF]

    def label_step(i, carry):
        put_turned(i, hit(i).astype(F32))
        return carry

    lax.fori_loop(0, ROWS // CH, label_step, 0)

    def part_cols(n):
        return pl.ds(pl.multiple_of(n * PART, PART), PART)

    def label_dot(n, carry):
        cols = part_cols(n)
        value = jnp.dot(g[...], w[:, cols], preferred_element_type=F32)
        els[:, cols] = value[: WIN // 2].astype(BF16)
        keepl[:, cols] = value[WIN // 2 :].astype(BF16)
        return carry

    lax.fori_loop(0, NPART, label_dot, 0)
    send("l", els, elr, elr, partner)
    arrived("l")

    def label_merge(j, carry):
        rows = pl.ds(pl.multiple_of(j * HALF, HALF), HALF)
        both = (keepl[rows, :].astype(F32) + elr[rows, :].astype(F32)).astype(BF16)
        rsla[j] = both[:QTR]
        for m in range(D // 128):
            hh, zz = m // NZ, m % NZ
            rows = pl.ds(pl.multiple_of(hh * TOK + j * QTR, QTR), QTR)
            rsl[zz, rows, :] = both[QTR:, m * 128 : (m + 1) * 128]
        return carry

    lax.fori_loop(0, NC, label_merge, 0)
    for d in FAR:
        to = (z + d) % NZ
        send(f"zl{d}", rsl.at[to], rl1.at[d], rl1.at[d], at_z(to))

    adv, length = sequence_terms(seq_ref[...], adv_ref)

    for i in range(3):
        arrived(f"a{i}")
        piece = win.at[half_rows(from_block[i], k), :]
        send(f"f{i}", piece, piece, win.at[half_rows(from_block[i], 1 - k), :], partner)
        spread_columns(i, from_block[i], piece)
    load_hid.wait()
    for i in range(3):
        arrived(f"f{i}")
    for d in FAR:
        to = (y + d) % NY
        src = rsla.at[to % NC, :, pl.ds(pl.multiple_of((to // NC) * (D // NH), D // NH), D // NH)]
        send(f"yk{d}", src, rk1.at[d], rk1.at[d], at_y(to))
    def block_rows(i):
        return pl.ds(pl.multiple_of(i * BLOCK, BLOCK), BLOCK)

    def logit_step(i, carry):
        logit[block_rows(i), :] = lax.dot_general(
            w[block_rows(i), :], win[...], (((1,), (1,)), ((), ())), preferred_element_type=F32
        )
        return carry

    lax.fori_loop(0, ROWS // BLOCK, logit_step, 0)

    def stat_step(i, carry):
        top, label = carry
        part = logit[rows_of(i), :]
        here = hit(i)
        top = jnp.maximum(top, jnp.max(jnp.where(here, -jnp.inf, part), axis=0, keepdims=True))
        label = label + jnp.sum(jnp.where(here, part, 0.0), axis=0, keepdims=True)
        return top, label

    top, label = lax.fori_loop(
        0, ROWS // CH, stat_step, (jnp.full((1, WIN), -jnp.inf, F32), jnp.zeros((1, WIN), F32))
    )

    def exp_step(i, total):
        here = hit(i)
        part = jnp.where(here, 0.0, jnp.exp(logit[rows_of(i), :] - top))
        q[0, rows_of(i), :] = jnp.where(here, -1.0, part).astype(BF16)
        put_turned(i, part)
        return total + jnp.sum(part, axis=0, keepdims=True)

    total = lax.fori_loop(0, ROWS // CH, exp_step, jnp.zeros((1, WIN), F32))
    put(st0, k, fold(top), fold(total), fold(label))
    send("c", st0.at[k], st0.at[k], st0.at[1 - k], partner)

    lo, hi = pl.ds(0, SPLIT), pl.ds(SPLIT, SPLIT)
    send("q1lo", q.at[0, lo, :], q.at[1, lo, :], q.at[1, lo, :], at_x(right))
    send("q2hi", q.at[0, hi, :], q.at[2, hi, :], q.at[2, hi, :], at_x(left))
    first = len(sent)

    def swap(n):
        return pltpu.make_async_remote_copy(
            src_ref=e1s.at[:, part_cols(n)],
            dst_ref=e1r.at[:, part_cols(n)],
            send_sem=send_sems.at[first + n],
            recv_sem=recv_sems.at[first + n],
            device_id=partner,
            device_id_type=MESH,
        )

    def weight_sums(n, carry):
        cols = part_cols(n)
        value = jnp.dot(g[...], w[:, cols], preferred_element_type=F32)
        e1s[:, cols] = value[: WIN // 2].astype(BF16)
        keep[:, cols] = value[WIN // 2 :]
        swap(n).start()
        return carry

    lax.fori_loop(0, NPART, weight_sums, 0)
    sent.extend(swap(n) for n in range(NPART))
    names.extend("e" for n in range(NPART))

    arrived("c")
    pair = merge(st0, 2)
    put(sty, y, *pair)
    put(stz, z, *pair)
    for d in FAR:
        send(f"cy{d}", sty.at[y], sty.at[y], sty.at[(y + NY - d) % NY], at_y((y + d) % NY))
    for d in FAR:
        send(f"cz{d}", stz.at[z], stz.at[z], stz.at[(z + NZ - d) % NZ], at_z((z + d) % NZ))

    def relative(ref, slot, norm):
        return unfold(jnp.exp(ref[slot, 0:2, :] - norm))

    turn([relative(st0, k, pair[0]), relative(st0, 1 - k, pair[0])], col0)

    def pair_merge(n, carry):
        cols = part_cols(n)
        swap(n).wait_recv()
        for j in range(NC):
            rows = slice(j * HALF, (j + 1) * HALF)
            factors = col0[half_rows(j, k), :]
            both = keep[rows, cols] * factors[:, 0:1] + e1r[rows, cols].astype(F32) * factors[:, 1:2]
            both = both.astype(BF16)
            rsa[j, :, cols] = both[:QTR]
            for m in range(PART // 128):
                hh, zz = n // (NPART // NH), n % (NPART // NH) * (PART // 128) + m
                rows_b = pl.ds(pl.multiple_of(hh * TOK + j * QTR, QTR), QTR)
                rsb[zz, rows_b, :] = both[QTR:, m * 128 : (m + 1) * 128]
        return carry

    lax.fori_loop(0, NPART, pair_merge, 0)

    for d in FAR:
        to = (y + d) % NY
        src = rsa.at[to % NC, :, pl.ds(pl.multiple_of((to // NC) * (D // NH), D // NH), D // NH)]
        send(f"ya{d}", src, ra1.at[d], ra1.at[d], at_y(to))
        to = (z + d) % NZ
        send(f"zb{d}", rsb.at[to], rb1.at[d], rb1.at[d], at_z(to))
    send("q1hi", q.at[0, hi, :], q.at[1, hi, :], q.at[1, hi, :], at_x(right))
    send("q2lo", q.at[0, lo, :], q.at[2, lo, :], q.at[2, lo, :], at_x(left))
    for d in range(1, NY):
        arrived(f"cy{d}")
    ring_y = merge(sty, NY)
    put(styz, z, *ring_y)
    for d in FAR:
        send(f"cyz{d}", styz.at[z], styz.at[z], styz.at[(z + NZ - d) % NZ], at_z((z + d) % NZ))
    for d in range(1, NZ):
        arrived(f"cz{d}")
    ring_z = merge(stz, NZ)
    put(stzy, y, *ring_z)
    for d in FAR:
        send(f"czy{d}", stzy.at[y], stzy.at[y], stzy.at[(y + NY - d) % NY], at_y((y + d) % NY))
    turn([relative(sty, (y + NY - d) % NY, ring_y[0]) for d in range(NY)], col1a)
    turn([relative(stz, (z + NZ - d) % NZ, ring_z[0]) for d in range(NZ)], col1b)

    arrived("q1lo")
    send("q3lo", q.at[1, lo, :], q.at[3, lo, :], q.at[3, lo, :], at_x(right))
    arrived("q2hi")
    send("q3hi", q.at[2, hi, :], q.at[3, hi, :], q.at[3, hi, :], at_x(left))
    own = rsl[z].astype(F32)
    for d in range(1, NZ):
        arrived(f"zl{d}")
        own = own + rl1[d].astype(F32)
    rl2s[...] = own.astype(BF16)
    for d in FAR:
        to = (y + d) % NY
        src = rl2s.at[pl.ds(pl.multiple_of((to // NC) * TOK + (to % NC) * QTR, QTR), QTR), :]
        send(f"yl{d}", src, rl2.at[d], rl2.at[d], at_y(to))
    own = rsla[c, :, pl.ds(pl.multiple_of(h * (D // NH), D // NH), D // NH)].astype(F32)
    for d in range(1, NY):
        arrived(f"yk{d}")
        own = own + rk1[d].astype(F32)
    rk2s[...] = own.astype(BF16)
    for d in FAR:
        to = (z + d) % NZ
        src = rk2s.at[:, pl.ds(pl.multiple_of(to * 128, 128), 128)]
        send(f"zk{d}", src, rk2.at[d], rk2.at[d], at_z(to))

    for i, number in ((3, c), (0, from_block[0]), (1, from_block[1]), (2, from_block[2])):
        for d in (1, 3, 2):
            arrived(f"h{i}{d}")
            piece = hc.at[place[d], half_rows(number, k), :]
            send(f"g{i}{d}", piece, piece, hc.at[place[d], half_rows(number, 1 - k), :], partner)
    hc[0] = win[:, pl.ds(pl.multiple_of(x * COLS, COLS), COLS)]

    settle(("q", "ya", "zb", "cyz", "czy", "yl", "zk", "g"))
    rows_a = pl.ds(pl.multiple_of(c * TOK + k * HALF, QTR), QTR)
    rows_b = pl.ds(pl.multiple_of(c * TOK + k * HALF + QTR, QTR), QTR)
    factors = col1a[rows_a, :]
    own = rsa[c, :, pl.ds(pl.multiple_of(h * (D // NH), D // NH), D // NH)].astype(F32) * factors[:, 0:1]
    for d in range(1, NY):
        arrived(f"ya{d}")
        own = own + ra1[d].astype(F32) * factors[:, d : d + 1]
    ra2s[...] = own.astype(BF16)
    for d in FAR:
        to = (z + d) % NZ
        src = ra2s.at[:, pl.ds(pl.multiple_of(to * 128, 128), 128)]
        send(f"za{d}", src, ra2.at[d], ra2.at[d], at_z(to))
    for d in range(1, NZ):
        arrived(f"cyz{d}")
    all_top, all_rest, all_label = merge(styz, NZ)
    peak = jnp.maximum(all_top, all_label)
    rest = all_rest * jnp.exp(all_top - peak)
    whole = rest + jnp.exp(all_label - peak)
    log_total = peak + jnp.log(whole)
    row_total = unfold(log_total)
    coeff = token_weights(
        unfold(all_label - log_total), mask_ref[...], adv, length, old_ref[...], refp_ref[...]
    )
    factor = coeff * jnp.exp(top - row_total)
    label_grad = coeff * unfold(rest / whole)
    put(scale, 0, fold(factor), fold(label_grad), fold(label_grad))
    for d in (1, 3, 2):
        send(f"x{d}", scale.at[0], scale.at[d], scale.at[d], at_x((x + d) % NX))

    factors = [
        col1b[pl.ds(pl.multiple_of(j * TOK + k * HALF + QTR, QTR), QTR), :] for j in range(NC)
    ]
    factors = jnp.concatenate(factors + factors, axis=0)
    own = rsb[z].astype(F32) * factors[:, 0:1]
    for d in range(1, NZ):
        arrived(f"zb{d}")
        own = own + rb1[d].astype(F32) * factors[:, d : d + 1]
    rb2s[...] = own.astype(BF16)
    for d in FAR:
        to = (y + d) % NY
        src = rb2s.at[pl.ds(pl.multiple_of((to // NC) * TOK + (to % NC) * QTR, QTR), QTR), :]
        send(f"yb{d}", src, rb2.at[d], rb2.at[d], at_y(to))
    settle(("q", "za", "yb", "x"))

    def form(slot, factor_row, label_row):
        def step(i, carry):
            part = q[slot, rows_of(i), :].astype(F32)
            grad = jnp.where(part < 0.0, label_row, -part * factor_row)
            gt[rows_of(i), slot * WIN : (slot + 1) * WIN] = grad.astype(BF16)
            return carry

        lax.fori_loop(0, ROWS // CH, step, 0)

    def rows_for(d):
        arrived(f"x{d}")
        return unfold(scale[d, 0:2, :]), unfold(scale[d, 2:4, :])

    form(0, factor, label_grad)
    for d in range(1, NY):
        arrived(f"czy{d}")
    turn([-coeff * relative(styz, (z + NZ - d) % NZ, log_total) for d in range(NZ)], col2a)
    turn([-coeff * relative(stzy, (y + NY - d) % NY, log_total) for d in range(NY)], col2b)
    turn([label_grad], coll)
    own = rk2s[:, pl.ds(pl.multiple_of(z * 128, 128), 128)].astype(F32)
    for d in range(1, NZ):
        arrived(f"zk{d}")
        own = own + rk2[d].astype(F32)
    other = rl2s[pl.ds(pl.multiple_of(h * TOK + c * QTR, QTR), QTR), :].astype(F32)
    for d in range(1, NY):
        arrived(f"yl{d}")
        other = other + rl2[d].astype(F32)
    own_label = jnp.concatenate([own, other], axis=0) * coll[half_rows(c, k), :][:, 0:1]

    for i in range(4):
        for d in (1, 3, 2):
            arrived(f"g{i}{d}")

    factors = col2a[rows_a, :]
    own = own_label[:QTR]
    own = own + ra2s[:, pl.ds(pl.multiple_of(z * 128, 128), 128)].astype(F32) * factors[:, 0:1]
    for d in range(1, NZ):
        arrived(f"za{d}")
        own = own + ra2[d].astype(F32) * factors[:, d : d + 1]
    fin[0, 0:QTR, :] = own.astype(BF16)
    factors = col2b[rows_b, :]
    own = own_label[QTR:]
    own = own + rb2s[pl.ds(pl.multiple_of(h * TOK + c * QTR, QTR), QTR), :].astype(F32) * factors[:, 0:1]
    for d in range(1, NY):
        arrived(f"yb{d}")
        own = own + rb2[d].astype(F32) * factors[:, d : d + 1]
    fin[0, QTR:HALF, :] = own.astype(BF16)
    send("fin", fin.at[0], fin.at[1], fin.at[1], partner)
    near = rows_for(1)
    arrived("q1hi")
    form(1, *near)
    near = rows_for(3)
    arrived("q2lo")
    form(2, *near)

    across = rows_for(2)
    arrived("q3lo")
    arrived("q3hi")
    form(3, *across)

    def head_step(i, carry):
        head_ref[block_rows(i), :] = jnp.dot(
            gt[block_rows(i), :], hc[...].reshape(NX * WIN, COLS), preferred_element_type=F32
        ).astype(BF16)
        return carry

    lax.fori_loop(0, ROWS // BLOCK, head_step, 0)

    arrived("fin")
    for slot, row in ((0, k), (1, 1 - k)):
        value = fin[slot].astype(F32)
        value = jnp.where(k == 0, value[:, :64], value[:, 64:])
        hg_ref[0, pl.ds(pl.multiple_of(row * HALF, HALF), HALF), :] = value.astype(BF16)
    drain()


def body(*args):
    vmem = pl.BlockSpec(memory_space=pltpu.VMEM)
    hbm = pl.BlockSpec(memory_space=pltpu.HBM)
    dma = pltpu.SemaphoreType.DMA
    args = [pltpu.with_memory_space_constraint(a, pltpu.HBM) for a in args]
    return pl.pallas_call(
        kernel,
        out_shape=(
            pltpu.VMEM((1, TOK, D // (NH * NZ * 2)), BF16),
            pltpu.VMEM((ROWS, COLS), BF16),
        ),
        in_specs=[hbm] * 8,
        out_specs=(vmem, vmem),
        scratch_shapes=[
            pltpu.VMEM((ROWS, D), BF16),
            pltpu.VMEM((WIN, D), BF16),
            pltpu.VMEM((NX, WIN, COLS), BF16),
            pltpu.VMEM((ROWS, WIN), F32),
            pltpu.VMEM((NX, ROWS, WIN), BF16),
            pltpu.VMEM((ROWS, NX * WIN), BF16),
            pltpu.VMEM((WIN, ROWS), BF16),
            pltpu.VMEM((WIN // 2, D), F32),
            pltpu.VMEM((WIN // 2, D), BF16),
            pltpu.VMEM((WIN // 2, D), BF16),
            pltpu.VMEM((WIN // 2, D), BF16),
            pltpu.VMEM((WIN // 2, D), BF16),
            pltpu.VMEM((WIN // 2, D), BF16),
            pltpu.VMEM((NC, QTR, D), BF16),
            pltpu.VMEM((NZ, NH * TOK, 128), BF16),
            pltpu.VMEM((NZ, NH * TOK, 128), BF16),
            pltpu.VMEM((NC, QTR, D), BF16),
            pltpu.VMEM((NY, QTR, D // NH), BF16),
            pltpu.VMEM((NZ, NH * TOK, 128), BF16),
            pltpu.VMEM((NZ, NH * TOK, 128), BF16),
            pltpu.VMEM((NY, QTR, D // NH), BF16),
            pltpu.VMEM((QTR, D // NH), BF16),
            pltpu.VMEM((NH * TOK, 128), BF16),
            pltpu.VMEM((NH * TOK, 128), BF16),
            pltpu.VMEM((QTR, D // NH), BF16),
            pltpu.VMEM((NZ, QTR, 128), BF16),
            pltpu.VMEM((NY, QTR, 128), BF16),
            pltpu.VMEM((NY, QTR, 128), BF16),
            pltpu.VMEM((NZ, QTR, 128), BF16),
            pltpu.VMEM((2, HALF, 128), BF16),
            pltpu.VMEM((2, 8, 128), F32),
            pltpu.VMEM((NY, 8, 128), F32),
            pltpu.VMEM((NZ, 8, 128), F32),
            pltpu.VMEM((NZ, 8, 128), F32),
            pltpu.VMEM((NY, 8, 128), F32),
            pltpu.VMEM((NX, 8, 128), F32),
            pltpu.VMEM((WIN, 8), F32),
            pltpu.VMEM((WIN, 8), F32),
            pltpu.VMEM((WIN, 8), F32),
            pltpu.VMEM((WIN, 8), F32),
            pltpu.VMEM((WIN, 8), F32),
            pltpu.VMEM((WIN, 8), F32),
            pltpu.VMEM((1, WIN), jnp.int32),
            pltpu.VMEM((1, WIN), jnp.int32),
            pltpu.VMEM((1, WIN), jnp.int32),
            pltpu.VMEM((1, WIN), F32),
            pltpu.VMEM((1, WIN), F32),
            pltpu.VMEM((1, 8), F32),
            dma((8,)),
            dma((SEMS,)),
            dma((SEMS,)),
        ],
        compiler_params=pltpu.CompilerParams(
            collective_id=0, has_side_effects=True, vmem_limit_bytes=48 * 1024 * 1024
        ),
        cost_estimate=pl.CostEstimate(
            flops=8 * WIN * D * ROWS, bytes_accessed=2 * ROWS * (D + COLS), transcendentals=4 * ROWS * WIN
        ),
    )(*args)


def solution(mesh):
    placed = (P("dp", "ctx", None), P(("ctx", "vocab"), None)) + (P("dp", None),) * 6
    return jax.shard_map(
        body,
        mesh=mesh,
        in_specs=placed,
        out_specs=(P("dp", "ctx", "vocab"), P(("ctx", "vocab"), "dp")),
        check_vma=False,
    )
```
